512 devices in a mesh: row: 32 (over y, x_lo, core), col: 16 (over z, x_hi).
Axes of the slice: x: 4 (x_hi: 2, x_lo: 2; x = x_hi * 2 + x_lo), y: 8, z: 8, core: 2. Of those that a mesh axis runs over, the one named last changes fastest.
Arguments:
- states: bfloat16 [32768, 512], P(('row', 'col')), may hold values from -1 to 1
- targets: float32 [32, 32768], P(None, ('row', 'col')), may hold values from -6 to 6
- start_coef: float32 [32, 32768], P(None, ('row', 'col')), may hold values from -4 to 4
- washout: int32 [32768], P(('row', 'col')), may hold values 0 or 1
Outputs:
- coef: float32 [32, 32768], P(None, ('row', 'col'))
- residual: float32 [32, 32768], P(None, ('row', 'col'))
The draws below stay inside these ranges and needn't reach their ends.
All inputs are finite; a program needn't handle non-finite values. No bound on the sum of `washout` on one device may be relied on, other than what follows from the above.
Results may differ from the reference program's by a relative error of at most 0.0003.
Values may be sent and summed in bfloat16 or wider, within the bound.
A program may use at most 64 MiB of HBM per device.

```python
import math
import jax
import jax.numpy as jnp
from jax import lax

DIM = 512
OUT = 32
SAMP_DEV = 64
SAMPLES = 32768


def draw_states(key, part):
    key = jax.random.fold_in(key, 11)
    keys = jax.random.split(key, 4)
    position = jnp.arange(SAMPLES, dtype=jnp.int32)
    step_table = jax.random.randint(keys[0], (4, 3), 3, 3000, dtype=jnp.int32)
    phase_table = jax.random.uniform(keys[1], (4, 3), jnp.float32, 0.0, 2.0 * math.pi)
    mixing = jax.random.normal(keys[2], (4, DIM), jnp.float32) * 1.25
    rough = jax.random.normal(keys[3], (SAMPLES, DIM), jnp.float32) * 0.25
    driven = rough
    for latent_index in range(4):
        signal = jnp.zeros((SAMPLES,), jnp.float32)
        for wave_index in range(3):
            turn = position * step_table[latent_index, wave_index] % 65536
            angle = turn.astype(jnp.float32) * (2.0 * math.pi / 65536.0) + phase_table[latent_index, wave_index]
            signal = signal + jnp.cos(angle)
        signal = signal * 0.8164966
        driven = driven + signal[:, None] * mixing[latent_index][None, :]
    return jnp.tanh(driven).astype(jnp.bfloat16)


def place_ends(values, key, smallest, largest):
    index_at = [jax.random.randint(jax.random.fold_in(key, axis), (), 0, length) for axis, length in enumerate(values.shape)]
    longest = values.shape.index(max(values.shape))
    beside = index_at[:longest] + [(index_at[longest] + 1) % values.shape[longest]] + index_at[longest + 1:]
    return values.at[tuple(index_at)].set(smallest).at[tuple(beside)].set(largest)


def levels(own_key, dims, cuts, smallest, top_value):
    loudness = 1.0
    for axis_at, shards_of in cuts:
        heights = jax.random.uniform(jax.random.fold_in(jax.random.fold_in(own_key, 6), axis_at), (shards_of,), jnp.float32, smallest / len(cuts), top_value / len(cuts))
        loudness = loudness * jnp.repeat(jnp.exp(heights), dims[axis_at] // shards_of).reshape((-1,) + (1,) * (len(dims) - 1 - axis_at))
    return loudness


def centred(rng, shape, spread, bound, cuts=(), kind=jnp.bfloat16):
    loudness = levels(rng, shape, cuts, -0.22, 0.18) if cuts else 1.0
    array = jax.random.normal(rng, shape, jnp.float32) * spread * loudness
    return jnp.minimum(jnp.maximum(array, -bound), bound).astype(kind)


def setup_inputs(seed: int = 0) -> dict:
    splits = jax.random.split(jax.random.key(seed), 5)
    return {
        "states": draw_states(jax.random.fold_in(splits[4], 71), 0),
        "targets": centred(splits[1], (OUT, SAMPLES), 1.0, 6.0, ((1, 512),), jnp.float32),
        "start_coef": centred(splits[2], (OUT, SAMPLES), 0.5, 4.0, ((1, 512),), jnp.float32),
        "washout": place_ends((jax.random.randint(splits[3], (SAMPLES,), 0, 8) < 7).astype(jnp.int32), jax.random.fold_in(splits[3], 1), 0, 1),
    }


ridge_value = 1.0


def apply_operator(vector, states_f, norms, mask):
    masked = vector * mask[None, :]
    blocks = states_f.shape[0] // SAMP_DEV

    def one_block(index):
        rows = lax.dynamic_slice_in_dim(states_f, index * SAMP_DEV, SAMP_DEV, 0)
        row_norm = lax.dynamic_slice_in_dim(norms, index * SAMP_DEV, SAMP_DEV, 0)
        cross = jnp.dot(rows, states_f.T, precision=lax.Precision.HIGHEST)
        tile = jnp.exp(-(row_norm[:, None] + norms[None, :] - 2.0 * cross) / DIM)
        return jnp.dot(masked, tile.T, precision=lax.Precision.HIGHEST)

    parts = lax.map(one_block, jnp.arange(blocks, dtype=jnp.int32))
    image = jnp.transpose(parts, (1, 0, 2)).reshape(vector.shape)
    return mask[None, :] * image + ridge_value * vector


def reference(states, targets, start_coef, washout):
    mask = washout.astype(jnp.float32)
    states_f = states.astype(jnp.float32)
    norms = jnp.sum(states_f * states_f, axis=1)
    start = mask[None, :] * targets - apply_operator(start_coef, states_f, norms, mask)
    image = apply_operator(start, states_f, norms, mask)
    squares = jnp.sum(start * start, axis=1)
    bending = jnp.sum(start * image, axis=1)
    alpha = squares / bending
    coef = start_coef + alpha[:, None] * start
    residual = start - alpha[:, None] * image
    return coef, residual
```

```python
import math

import jax
import jax.numpy as jnp
from jax import lax
from jax.experimental import pallas as pl
from jax.experimental.pallas import tpu as pltpu
from jax.sharding import PartitionSpec as P

MESH = pl.DeviceIdType.MESH
RING = 8
SAMP = 64
DIM = 512
OUT = 32
ROUNDS = 8
EXP_SCALE = math.log2(math.e) * 2.0 / DIM


def offsets(n, j):
    if n == 0:
        return 0, j
    if n == 7:
        return 4, j
    k, a = (n + 1) // 2, (n - 1) % 2
    return (RING - k if j == 0 else k), a


def mirror(n, j):
    return j if n in (0, 7) else 1 - j


def lane_group():
    return lax.broadcasted_iota(jnp.int32, (16, 128), 1) // OUT


def by_group(pieces):
    group = lane_group()
    out = pieces[3]
    for g in (2, 1, 0):
        out = jnp.where(group == g, pieces[g], out)
    return out


def pack(block, at):
    return by_group(
        [
            pltpu.roll(block[16 * g : 16 * g + 16], (OUT * (g - at)) % 128, axis=1)
            if g != at
            else block[16 * g : 16 * g + 16]
            for g in range(4)
        ]
    )


def fold_lanes(x):
    x = x + pltpu.roll(x, 64, axis=1)
    return x + pltpu.roll(x, 32, axis=1)


def kernel(
    states, targets, start_coef, washout,
    coef_out, res_out,
    col_st, row_st, e_hi, e_lo, w_all, flip,
    vec0, part1, got1, vec1, vec1r, part2, got2, dots, got_dots,
    send_sem, sib_send, c_recv, s_recv, r_recv, v_recv, vs_recv, phase_recv,
):
    row, col = lax.axis_index("row"), lax.axis_index("col")
    core, xl, y = row % 2, (row // 2) % 2, row // 4
    xh, z = col % 2, col // 2

    def row_peer(dy, dxl, dcore):
        return (((y + dy) % RING * 2 + (xl + dxl) % 2) * 2 + (core + dcore) % 2, col)

    def col_peer(dz, dxh):
        return (row, (z + dz) % RING * 2 + (xh + dxh) % 2)

    y_up, y_down = row_peer(1, 0, 0), row_peer(RING - 1, 0, 0)
    z_up, z_down = col_peer(1, 0), col_peer(RING - 1, 0)
    x_near, sibling, x_far = row_peer(0, 1, 0), row_peer(0, 0, 1), col_peer(0, 1)
    near = (y_up, y_down, z_up, z_down, x_near, sibling, x_far)

    barrier = pltpu.get_barrier_semaphore()
    for who in near:
        pl.semaphore_signal(barrier, inc=1, device_id=who, device_id_type=MESH)
    pl.semaphore_wait(barrier, len(near))

    def send(src, dst, to, s_sem, r_sem):
        pltpu.make_async_remote_copy(
            src_ref=src, dst_ref=dst, send_sem=s_sem, recv_sem=r_sem, device_id=to, device_id_type=MESH
        ).start()

    def wait(ref, sem):
        pltpu.make_async_copy(ref, ref, sem).wait()

    def c_slot(n, j):
        return 4 * n + j

    def r_slot(n, j):
        return 2 * n + j

    def send_c(src, n, j, to):
        send(src, col_st.at[c_slot(n, j)], to, send_sem.at[0], c_recv.at[r_slot(n, j)])

    def send_r(src, n, j, to):
        send(src, row_st.at[r_slot(n, j)], to, send_sem.at[1], r_recv.at[r_slot(n, j)])

    def send_v(src, n, j, to):
        send(src, vec0.at[c_slot(n, j)], to, send_sem.at[2], v_recv.at[r_slot(n, j)])

    send_c(states, 1, 0, y_up)
    send_c(states, 1, 1, y_down)
    send_r(states, 1, 0, z_up)
    send_r(states, 1, 1, z_down)
    send_c(states, 0, 1, x_near)
    send_r(states, 0, 1, x_far)
    col_st[0] = states[...]
    row_st[0] = states[...]

    own_f = states[...].astype(jnp.float32)
    norm = jnp.sum(own_f * own_f, axis=1, keepdims=True)
    damp_col = jnp.broadcast_to(jnp.exp(norm * (-1.0 / DIM)), (SAMP, 128))
    damp = by_group([damp_col[16 * g : 16 * g + 16] for g in range(4)])
    flip[...] = jnp.zeros((128, 128), jnp.float32)
    flip[0:OUT, 0:SAMP] = targets[...]
    flip[OUT : 2 * OUT, 0:SAMP] = start_coef[...]
    flip[2 * OUT : 3 * OUT, 0:SAMP] = jnp.broadcast_to(washout[...].astype(jnp.float32), (OUT, SAMP))
    turned = flip[...].T[0:SAMP]
    mask = pack(turned, 2)
    target = pack(turned, 0) * mask
    start = pack(turned, 1)
    scale = mask * damp
    vec0[0] = scale * start

    send_v(vec0.at[0], 1, 0, y_up)
    send_v(vec0.at[0], 1, 1, y_down)
    send_v(vec0.at[0], 0, 1, x_near)

    def pass_on(n):
        if n == 0:
            wait(col_st.at[1], c_recv.at[1])
            send_c(col_st.at[1], 2, 0, y_up)
            send_c(col_st.at[1], 2, 1, y_down)
            wait(row_st.at[1], r_recv.at[1])
            send_r(row_st.at[1], 2, 0, z_up)
            send_r(row_st.at[1], 2, 1, z_down)
            wait(vec0.at[1], v_recv.at[1])
            send_v(vec0.at[1], 2, 0, y_up)
            send_v(vec0.at[1], 2, 1, y_down)
        else:
            for j in (0, 1):
                to_y, to_z = (y_up, z_up) if j == 0 else (y_down, z_down)
                after = n + 2 if n < 5 else 7
                go = n < 5 or (n == 5 and j == 0) or (n == 6 and j == 1)
                wait(col_st.at[c_slot(n, j)], c_recv.at[r_slot(n, j)])
                if go:
                    send_c(col_st.at[c_slot(n, j)], after, j, to_y)
                wait(row_st.at[r_slot(n, j)], r_recv.at[r_slot(n, j)])
                if go:
                    send_r(row_st.at[r_slot(n, j)], after, j, to_z)
                wait(vec0.at[c_slot(n, j)], v_recv.at[r_slot(n, j)])
                if go:
                    send_v(vec0.at[c_slot(n, j)], after, j, to_y)
        own, other = pl.ds(4 * n, 2), pl.ds(4 * n + 2, 2)
        send(col_st.at[own], col_st.at[other], sibling, sib_send.at[0], s_recv.at[n])
        send(vec0.at[own], vec0.at[other], sibling, sib_send.at[1], vs_recv.at[n])

    def block(rows, r_at, columns, c_at, r_count, c_count):
        left = row_st[r_at : r_at + r_count].reshape(r_count * SAMP, DIM)
        right = col_st[c_at : c_at + c_count].reshape(c_count * SAMP, DIM)
        cross = lax.dot_general(left, right, (((1,), (1,)), ((), ())), preferred_element_type=jnp.float32)
        e = jnp.exp2(cross * EXP_SCALE)
        hi = e.astype(jnp.bfloat16)
        e_hi[rows, columns] = hi
        e_lo[rows, columns] = (e - hi.astype(jnp.float32)).astype(jnp.bfloat16)

    def compute(n):
        other = pl.ds(4 * n + 2, 2)
        wait(col_st.at[other], s_recv.at[n])
        columns = pl.ds(256 * n, 256)
        for at in range(n + 1):
            block(pl.ds(128 * at, 128), 2 * at, columns, 4 * n, 2, 4)
        for at in range(n):
            block(pl.ds(128 * n, 128), 2 * n, pl.ds(256 * at, 256), 4 * at, 2, 4)

    for n in range(ROUNDS):
        pass_on(n)
        if n >= 1:
            compute(n - 1)
    compute(ROUNDS - 1)
    for n in range(ROUNDS):
        wait(vec0.at[pl.ds(4 * n + 2, 2)], vs_recv.at[n])

    group = lane_group()

    def spread(vec):
        def one(s, carry):
            v = vec[s, 0:16, :]
            hi = v.astype(jnp.bfloat16).astype(jnp.float32)
            lo = v - hi
            at = pl.multiple_of(s * SAMP, SAMP)
            for g in range(4):
                keep = group == g
                w_all[pl.ds(at + 16 * g, 16), 0:128] = jnp.where(keep, hi, 0.0).astype(jnp.bfloat16)
                w_all[pl.ds(at + 16 * g, 16), 128:256] = jnp.where(keep, lo, 0.0).astype(jnp.bfloat16)
            return carry

        lax.fori_loop(0, 32, one, 0)

    def apply(part):
        for chunk in range(4):
            rows = pl.ds(256 * chunk, 256)
            both = jnp.dot(e_hi[rows, :], w_all[...], preferred_element_type=jnp.float32)
            low = jnp.dot(e_lo[rows, :], w_all[:, 0:128], preferred_element_type=jnp.float32)
            acc = fold_lanes(both[:, 0:128] + both[:, 128:256] + low)
            for s in range(4):
                part[4 * chunk + s, 0:16, :] = by_group(
                    [acc[64 * s + 16 * g : 64 * s + 16 * g + 16] for g in range(4)]
                )

    row_slots = [(n, j) for n in range(ROUNDS) for j in (0, 1)]

    def to_owners(part, got, s_sem, r_sem):
        for n, j in row_slots[1:]:
            dz, dxh = offsets(n, j)
            send(part.at[r_slot(n, j)], got.at[r_slot(n, mirror(n, j))], col_peer(dz, dxh), s_sem, r_sem)

    spread(vec0)
    apply(part1)
    to_owners(part1, got1, send_sem.at[3], phase_recv.at[0])
    wait(got1.at[pl.ds(1, 15)], phase_recv.at[0])
    total = part1[0]
    for s in range(1, 16):
        total = total + got1[s]
    r0 = target - (scale * total + start)
    weight = scale * r0
    squares = jnp.broadcast_to(jnp.sum(r0 * r0, axis=0, keepdims=True), (8, 128))
    vec1[0, 0:16, :] = weight
    vec1[0, 16:24, :] = squares
    vec1r[0] = weight

    for n, j in row_slots:
        dy, dxl = offsets(n, j)
        for dcore in (0, 1):
            if (n, j, dcore) == (0, 0, 0):
                continue
            at = 4 * n + 2 * dcore + mirror(n, j)
            send(vec1.at[0], vec1.at[at], row_peer(dy, dxl, dcore), send_sem.at[4], phase_recv.at[1])
    for n, j in row_slots[1:]:
        dz, dxh = offsets(n, j)
        send(vec1r.at[0], vec1r.at[r_slot(n, mirror(n, j))], col_peer(dz, dxh), send_sem.at[5], phase_recv.at[2])
    wait(vec1.at[pl.ds(1, 31)], phase_recv.at[1])
    spread(vec1)
    apply(part2)
    wait(vec1r.at[pl.ds(1, 15)], phase_recv.at[2])
    bend = vec1r[0] * part2[0, 0:16, :]
    for s in range(1, 16):
        bend = bend + vec1r[s] * part2[s, 0:16, :]
    bend = jnp.sum(bend, axis=0, keepdims=True)
    sq = vec1[0, 16:24, :]
    for s in range(1, 32):
        sq = sq + vec1[s, 16:24, :]
    tail = jnp.where(lax.broadcasted_iota(jnp.int32, (8, 128), 0) == 0, jnp.broadcast_to(bend, (8, 128)), sq)
    for s in range(16):
        part2[s, 16:24, :] = tail
    to_owners(part2, got2, send_sem.at[6], phase_recv.at[3])
    wait(got2.at[pl.ds(1, 15)], phase_recv.at[3])
    total = part2[0]
    for s in range(1, 16):
        total = total + got2[s]
    q = scale * total[0:16] + r0
    tail = total[16:24]
    dots[...] = tail
    for n, j in row_slots:
        dy, dxl = offsets(n, j)
        for dcore in (0, 1):
            if (n, j, dcore) == (0, 0, 0):
                continue
            at = 4 * n + 2 * dcore + mirror(n, j)
            send(dots, got_dots.at[at], row_peer(dy, dxl, dcore), send_sem.at[7], phase_recv.at[4])
    wait(got_dots.at[pl.ds(1, 31)], phase_recv.at[4])
    bend = tail
    for s in range(1, 32):
        bend = bend + got_dots[s]
    squares = fold_lanes(tail)[1:2]
    bend = fold_lanes(bend)[0:1] + squares
    alpha = squares / bend
    coef = start + alpha * r0
    res = r0 - alpha * q
    flip[...] = jnp.zeros((128, 128), jnp.float32)
    low = lax.broadcasted_iota(jnp.int32, (16, 128), 1) < OUT
    for g in range(4):
        a = pltpu.roll(coef, (128 - OUT * g) % 128, axis=1) if g else coef
        b = pltpu.roll(res, (128 + OUT - OUT * g) % 128, axis=1) if g != 1 else res
        flip[16 * g : 16 * g + 16, :] = jnp.where(low, a, b)
    back = flip[...].T
    coef_out[...] = back[0:OUT, 0:SAMP]
    res_out[...] = back[OUT : 2 * OUT, 0:SAMP]

    wait(col_st.at[pl.ds(0, 15)], send_sem.at[0])
    wait(row_st.at[pl.ds(0, 15)], send_sem.at[1])
    wait(vec0.at[pl.ds(0, 15)], send_sem.at[2])
    wait(col_st.at[pl.ds(0, 16)], sib_send.at[0])
    wait(vec0.at[pl.ds(0, 16)], sib_send.at[1])
    wait(part1.at[pl.ds(0, 15)], send_sem.at[3])
    wait(vec1.at[pl.ds(0, 31)], send_sem.at[4])
    wait(vec1r.at[pl.ds(0, 15)], send_sem.at[5])
    wait(part2.at[pl.ds(0, 15)], send_sem.at[6])
    wait(got_dots.at[pl.ds(0, 31)], send_sem.at[7])


def local(states, targets, start_coef, washout):
    f32, bf16 = jnp.float32, jnp.bfloat16
    vmem = pl.BlockSpec(memory_space=pltpu.VMEM)
    out = jax.ShapeDtypeStruct((OUT, SAMP), f32)
    return pl.pallas_call(
        kernel,
        out_shape=(out, out),
        in_specs=[vmem] * 4,
        out_specs=(vmem, vmem),
        scratch_shapes=[
            pltpu.VMEM((32, SAMP, DIM), bf16),
            pltpu.VMEM((16, SAMP, DIM), bf16),
            pltpu.VMEM((1024, 2048), bf16),
            pltpu.VMEM((1024, 2048), bf16),
            pltpu.VMEM((2048, 256), bf16),
            pltpu.VMEM((128, 128), f32),
            pltpu.VMEM((32, 16, 128), f32),
            pltpu.VMEM((16, 16, 128), f32),
            pltpu.VMEM((16, 16, 128), f32),
            pltpu.VMEM((32, 24, 128), f32),
            pltpu.VMEM((16, 16, 128), f32),
            pltpu.VMEM((16, 24, 128), f32),
            pltpu.VMEM((16, 24, 128), f32),
            pltpu.VMEM((8, 128), f32),
            pltpu.VMEM((32, 8, 128), f32),
            pltpu.SemaphoreType.DMA((8,)),
            pltpu.SemaphoreType.DMA((2,)),
            pltpu.SemaphoreType.DMA((16,)),
            pltpu.SemaphoreType.DMA((8,)),
            pltpu.SemaphoreType.DMA((16,)),
            pltpu.SemaphoreType.DMA((16,)),
            pltpu.SemaphoreType.DMA((8,)),
            pltpu.SemaphoreType.DMA((5,)),
        ],
        compiler_params=pltpu.CompilerParams(
            collective_id=0, has_side_effects=True, vmem_limit_bytes=48 * 1024 * 1024
        ),
    )(states, targets, start_coef, washout.reshape(1, SAMP))


def solution(mesh):
    return jax.shard_map(
        local,
        mesh=mesh,
        in_specs=(
            P(("row", "col"), None),
            P(None, ("row", "col")),
            P(None, ("row", "col")),
            P(("row", "col")),
        ),
        out_specs=(P(None, ("row", "col")), P(None, ("row", "col"))),
        check_vma=False,
    )
```

```python
import math

import jax
import jax.numpy as jnp
from jax import lax
from jax.experimental import pallas as pl
from jax.experimental.pallas import tpu as pltpu
from jax.sharding import PartitionSpec as P

MESH = pl.DeviceIdType.MESH
RING = 8
SAMP = 64
DIM = 512
OUT = 32
ROUNDS = 8
EXP_SCALE = math.log2(math.e) * 2.0 / DIM


def offsets(n, j):
    if n == 0:
        return 0, j
    if n == 7:
        return 4, j
    k, a = (n + 1) // 2, (n - 1) % 2
    return (RING - k if j == 0 else k), a


def mirror(n, j):
    return j if n in (0, 7) else 1 - j


def lane_group():
    return lax.broadcasted_iota(jnp.int32, (16, 128), 1) // OUT


def by_group(pieces):
    group = lane_group()
    out = pieces[3]
    for g in (2, 1, 0):
        out = jnp.where(group == g, pieces[g], out)
    return out


def pack(block, at):
    return by_group(
        [
            pltpu.roll(block[16 * g : 16 * g + 16], (OUT * (g - at)) % 128, axis=1)
            if g != at
            else block[16 * g : 16 * g + 16]
            for g in range(4)
        ]
    )


def fold_lanes(x):
    x = x + pltpu.roll(x, 64, axis=1)
    return x + pltpu.roll(x, 32, axis=1)


def kernel(
    states_in, targets_in, coef_in, washout_in,
    coef_out, res_out,
    states, vectors, washout, col_st, row_st, e_hi, e_lo, w_all, acc, flip,
    vec0, part1, got1, vec1, vec1r, part2, got2, dots, got_dots, got_dots2,
    in_sem, send_sem, sib_send, c_recv, s_recv, r_recv, v_recv, vs_recv, phase_recv,
):
    row, col = lax.axis_index("row"), lax.axis_index("col")
    core, xl, y = row % 2, (row // 2) % 2, row // 4
    xh, z = col % 2, col // 2

    def row_peer(dy, dxl, dcore):
        return (((y + dy) % RING * 2 + (xl + dxl) % 2) * 2 + (core + dcore) % 2, col)

    def col_peer(dz, dxh):
        return (row, (z + dz) % RING * 2 + (xh + dxh) % 2)

    y_up, y_down = row_peer(1, 0, 0), row_peer(RING - 1, 0, 0)
    z_up, z_down = col_peer(1, 0), col_peer(RING - 1, 0)
    x_near, sibling, x_far = row_peer(0, 1, 0), row_peer(0, 0, 1), col_peer(0, 1)
    near = (y_up, y_down, z_up, z_down, x_near, sibling, x_far)

    barrier = pltpu.get_barrier_semaphore()
    for who in near:
        pl.semaphore_signal(barrier, inc=1, device_id=who, device_id_type=MESH)

    fetches = [
        pltpu.make_async_copy(states_in, states, in_sem.at[0]),
        pltpu.make_async_copy(targets_in, vectors.at[0], in_sem.at[1]),
        pltpu.make_async_copy(coef_in, vectors.at[1], in_sem.at[2]),
        pltpu.make_async_copy(washout_in, washout, in_sem.at[3]),
    ]
    for fetch in fetches:
        fetch.start()
    fetches[0].wait()
    pl.semaphore_wait(barrier, len(near))

    def send(src, dst, to, s_sem, r_sem):
        pltpu.make_async_remote_copy(
            src_ref=src, dst_ref=dst, send_sem=s_sem, recv_sem=r_sem, device_id=to, device_id_type=MESH
        ).start()

    def wait(ref, sem):
        pltpu.make_async_copy(ref, ref, sem).wait()

    def slot(n, j):
        return 2 * n + j

    def send_c(src, n, j, to):
        send(src, col_st.at[slot(n, j)], to, send_sem.at[0], c_recv.at[slot(n, j)])

    def send_r(src, n, j, to):
        send(src, row_st.at[slot(n, j)], to, send_sem.at[1], r_recv.at[slot(n, j)])

    def send_v(src, n, j, to):
        send(src, vec0.at[slot(n, j)], to, send_sem.at[2], v_recv.at[slot(n, j)])

    send_c(states, 1, 0, y_up)
    send_c(states, 1, 1, y_down)
    send_r(states, 1, 0, z_up)
    send_r(states, 1, 1, z_down)
    send_r(states, 0, 1, x_far)
    send_c(states, 0, 1, x_near)
    col_st[0] = states[...]
    row_st[0] = states[...]

    own_f = states[...].astype(jnp.float32)
    norm = jnp.sum(own_f * own_f, axis=1, keepdims=True)
    damp_col = jnp.broadcast_to(jnp.exp(norm * (-1.0 / DIM)), (SAMP, 128))
    damp = by_group([damp_col[16 * g : 16 * g + 16] for g in range(4)])
    for fetch in fetches[1:]:
        fetch.wait()
    flip[0:OUT, 0:SAMP] = vectors[0]
    flip[OUT : 2 * OUT, 0:SAMP] = vectors[1]
    flip[2 * OUT : 3 * OUT, 0:SAMP] = jnp.broadcast_to(washout[...].astype(jnp.float32), (OUT, SAMP))
    turned = flip[...].T[0:SAMP]
    mask = pack(turned, 2)
    target = pack(turned, 0) * mask
    start = pack(turned, 1)
    scale = mask * damp
    vec0[0] = scale * start

    send_v(vec0.at[0], 1, 0, y_up)
    send_v(vec0.at[0], 1, 1, y_down)
    send_v(vec0.at[0], 0, 1, x_near)

    def pass_states(n):
        if n == 0:
            wait(row_st.at[1], r_recv.at[1])
            send_r(row_st.at[1], 2, 0, z_up)
            send_r(row_st.at[1], 2, 1, z_down)
            wait(col_st.at[1], c_recv.at[1])
            send_c(col_st.at[1], 2, 0, y_up)
            send_c(col_st.at[1], 2, 1, y_down)
        else:
            for j in (0, 1):
                to_y, to_z = (y_up, z_up) if j == 0 else (y_down, z_down)
                after = n + 2 if n < 5 else 7
                go = n < 5 or (n == 5 and j == 0) or (n == 6 and j == 1)
                wait(row_st.at[slot(n, j)], r_recv.at[slot(n, j)])
                if go:
                    send_r(row_st.at[slot(n, j)], after, j, to_z)
                wait(col_st.at[slot(n, j)], c_recv.at[slot(n, j)])
                if go:
                    send_c(col_st.at[slot(n, j)], after, j, to_y)
        send(
            col_st.at[pl.ds(2 * n, 2)], col_st.at[pl.ds(16 + 2 * n, 2)], sibling, sib_send.at[0], s_recv.at[n]
        )

    def pass_vectors(n):
        if n == 0:
            wait(vec0.at[1], v_recv.at[1])
            send_v(vec0.at[1], 2, 0, y_up)
            send_v(vec0.at[1], 2, 1, y_down)
        else:
            for j in (0, 1):
                to_y = y_up if j == 0 else y_down
                after = n + 2 if n < 5 else 7
                go = n < 5 or (n == 5 and j == 0) or (n == 6 and j == 1)
                wait(vec0.at[slot(n, j)], v_recv.at[slot(n, j)])
                if go:
                    send_v(vec0.at[slot(n, j)], after, j, to_y)
        send(vec0.at[pl.ds(2 * n, 2)], vec0.at[pl.ds(16 + 2 * n, 2)], sibling, sib_send.at[1], vs_recv.at[n])

    group = lane_group()

    def spread(vec, first, count):
        for s in range(first, first + count):
            v = vec[s]
            hi = v.astype(jnp.bfloat16).astype(jnp.float32)
            lo = v - hi
            for g in range(4):
                keep = group == g
                at = SAMP * s + 16 * g
                w_all[at : at + 16, 0:128] = jnp.where(keep, hi, 0.0).astype(jnp.bfloat16)
                w_all[at : at + 16, 128:256] = jnp.where(keep, lo, 0.0).astype(jnp.bfloat16)

    def product(hi, lo, w):
        both = jnp.dot(hi, w, preferred_element_type=jnp.float32)
        low = jnp.dot(lo, w[:, 0:128], preferred_element_type=jnp.float32)
        return both[:, 0:128] + both[:, 128:256] + low

    def tile(r_first, r_count, ranges, fresh):
        left = row_st[r_first : r_first + r_count].reshape(r_count * SAMP, DIM)
        right = jnp.concatenate([col_st[a : a + k].reshape(k * SAMP, DIM) for a, k in ranges], axis=0)
        w = jnp.concatenate([w_all[a * SAMP : (a + k) * SAMP] for a, k in ranges], axis=0)
        cross = lax.dot_general(left, right, (((1,), (1,)), ((), ())), preferred_element_type=jnp.float32)
        e = jnp.exp2(cross * EXP_SCALE)
        hi = e.astype(jnp.bfloat16)
        lo = (e - hi.astype(jnp.float32)).astype(jnp.bfloat16)
        rows = pl.ds(r_first * SAMP, r_count * SAMP)
        at = 0
        for a, k in ranges:
            columns = pl.ds(a * SAMP, k * SAMP)
            e_hi[rows, columns] = hi[:, at : at + k * SAMP]
            e_lo[rows, columns] = lo[:, at : at + k * SAMP]
            at += k * SAMP
        add = product(hi, lo, w)
        acc[rows, :] = add if fresh else acc[rows, :] + add

    def compute(n, rounds):
        for k in range(n, n + rounds):
            wait(col_st.at[pl.ds(16 + 2 * k, 2)], s_recv.at[k])
            wait(vec0.at[pl.ds(16 + 2 * k, 2)], vs_recv.at[k])
        spread(vec0, 2 * n, 2 * rounds)
        spread(vec0, 16 + 2 * n, 2 * rounds)
        new = [(2 * n, 2 * rounds), (16 + 2 * n, 2 * rounds)]
        if n:
            tile(0, 2 * n, new, False)
            tile(2 * n, 2 * rounds, [(0, 2 * n + 2 * rounds), (16, 2 * n + 2 * rounds)], True)
        else:
            tile(0, 2 * rounds, new, True)

    pass_states(0)
    pass_states(1)
    pass_vectors(0)
    pass_vectors(1)
    compute(0, 2)
    pass_states(2)
    pass_states(3)
    pass_vectors(2)
    pass_vectors(3)
    compute(2, 2)
    pass_states(4)
    pass_states(5)
    pass_vectors(4)
    pass_vectors(5)
    compute(4, 2)
    pass_states(6)
    pass_vectors(6)
    compute(6, 1)
    pass_states(7)
    pass_vectors(7)
    compute(7, 1)

    row_slots = [(n, j) for n in range(ROUNDS) for j in (0, 1)]
    far_first = row_slots[::-1]

    def to_owner(part, got, n, j, s_sem, r_sem):
        s = slot(n, j)
        whole = fold_lanes(acc[SAMP * s : SAMP * s + SAMP, :])
        part[s] = by_group([whole[16 * g : 16 * g + 16] for g in range(4)])
        if s:
            dz, dxh = offsets(n, j)
            send(part.at[s], got.at[slot(n, mirror(n, j))], col_peer(dz, dxh), s_sem, r_sem)

    for n, j in far_first:
        to_owner(part1, got1, n, j, send_sem.at[3], phase_recv.at[0])
    wait(got1.at[pl.ds(1, 15)], phase_recv.at[0])
    total = part1[0]
    for s in range(1, 16):
        total = total + got1[s]
    r0 = target - (scale * total + start)
    weight = scale * r0
    vec1[0] = weight
    vec1r[0] = weight

    for n, j in far_first[:-1]:
        dy, dxl = offsets(n, j)
        at = slot(n, mirror(n, j))
        send(vec1.at[0], vec1.at[at], row_peer(dy, dxl, 0), send_sem.at[4], phase_recv.at[1 if n < 4 else 2])
    send(vec1.at[0], vec1.at[16], sibling, sib_send.at[2], phase_recv.at[3])
    for n, j in far_first[:-1]:
        dz, dxh = offsets(n, j)
        send(vec1r.at[0], vec1r.at[slot(n, mirror(n, j))], col_peer(dz, dxh), send_sem.at[5], phase_recv.at[6])

    def second(first, count, fresh, rows):
        columns = pl.ds(first * SAMP, count * SAMP)
        add = product(e_hi[rows, columns], e_lo[rows, columns], w_all[columns, :])
        acc[rows, :] = add if fresh else acc[rows, :] + add

    every = pl.ds(0, 1024)
    wait(vec1.at[pl.ds(1, 7)], phase_recv.at[1])
    send(vec1.at[pl.ds(1, 7)], vec1.at[pl.ds(17, 7)], sibling, sib_send.at[2], phase_recv.at[4])
    spread(vec1, 0, 8)
    second(0, 8, True, every)
    wait(vec1.at[pl.ds(8, 8)], phase_recv.at[2])
    send(vec1.at[pl.ds(8, 8)], vec1.at[pl.ds(24, 8)], sibling, sib_send.at[2], phase_recv.at[5])
    spread(vec1, 8, 8)
    second(8, 8, False, every)
    wait(vec1.at[16], phase_recv.at[3])
    wait(vec1.at[pl.ds(17, 7)], phase_recv.at[4])
    spread(vec1, 16, 8)
    second(16, 8, False, every)
    wait(vec1.at[pl.ds(24, 8)], phase_recv.at[5])
    spread(vec1, 24, 8)
    for chunk in (3, 2, 1, 0):
        second(24, 8, False, pl.ds(256 * chunk, 256))
        for n, j in far_first[12 - 4 * chunk : 16 - 4 * chunk]:
            to_owner(part2, got2, n, j, send_sem.at[6], phase_recv.at[7])

    wait(vec1r.at[pl.ds(1, 15)], phase_recv.at[6])
    bend = vec1r[0] * part2[0]
    for s in range(1, 16):
        bend = bend + vec1r[s] * part2[s]
    bend = jnp.sum(bend, axis=0, keepdims=True)
    squares = jnp.sum(r0 * r0, axis=0, keepdims=True)
    first_row = lax.broadcasted_iota(jnp.int32, (8, 128), 0) == 0
    both = fold_lanes(jnp.where(first_row, jnp.broadcast_to(bend, (8, 128)), jnp.broadcast_to(squares, (8, 128))))
    dots[0] = both
    two = pl.ds(0, 2)
    for n, j in far_first:
        dy, dxl = offsets(n, j)
        for dcore in (1, 0):
            if (n, j, dcore) != (0, 0, 0):
                at = 16 * dcore + slot(n, mirror(n, j))
                send(
                    dots.at[0, two], got_dots.at[at, two], row_peer(dy, dxl, dcore), send_sem.at[7], phase_recv.at[8]
                )
    wait(got_dots.at[pl.ds(1, 31), two], phase_recv.at[8])
    both = both[0:2]
    for s in range(1, 32):
        both = both + got_dots[s, 0:2, :]
    dots[1, 0:2, :] = both
    for n, j in far_first[:-1]:
        dz, dxh = offsets(n, j)
        at = slot(n, mirror(n, j))
        send(dots.at[1, two], got_dots2.at[at, two], col_peer(dz, dxh), send_sem.at[8], phase_recv.at[9])
    wait(got2.at[pl.ds(1, 15)], phase_recv.at[7])
    total = part2[0]
    for s in range(1, 16):
        total = total + got2[s]
    q = scale * total + r0
    wait(got_dots2.at[pl.ds(1, 15), two], phase_recv.at[9])
    for s in range(1, 16):
        both = both + got_dots2[s, 0:2, :]
    squares = both[1:2]
    alpha = squares / (both[0:1] + squares)
    coef = start + alpha * r0
    res = r0 - alpha * q
    low = lax.broadcasted_iota(jnp.int32, (16, 128), 1) < OUT
    for g in range(4):
        a = pltpu.roll(coef, (128 - OUT * g) % 128, axis=1) if g else coef
        b = pltpu.roll(res, (128 + OUT - OUT * g) % 128, axis=1) if g != 1 else res
        flip[16 * g : 16 * g + 16, :] = jnp.where(low, a, b)
    back = flip[...].T
    coef_out[...] = back[0:OUT, 0:SAMP]
    res_out[...] = back[OUT : 2 * OUT, 0:SAMP]

    wait(col_st.at[pl.ds(0, 15)], send_sem.at[0])
    wait(row_st.at[pl.ds(0, 15)], send_sem.at[1])
    wait(vec0.at[pl.ds(0, 15)], send_sem.at[2])
    wait(col_st.at[pl.ds(0, 16)], sib_send.at[0])
    wait(vec0.at[pl.ds(0, 16)], sib_send.at[1])
    wait(vec1.at[pl.ds(0, 16)], sib_send.at[2])
    wait(part1.at[pl.ds(0, 15)], send_sem.at[3])
    wait(vec1.at[pl.ds(0, 15)], send_sem.at[4])
    wait(vec1r.at[pl.ds(0, 15)], send_sem.at[5])
    wait(part2.at[pl.ds(0, 15)], send_sem.at[6])
    wait(got_dots.at[pl.ds(0, 31), two], send_sem.at[7])
    wait(got_dots2.at[pl.ds(0, 15), two], send_sem.at[8])


def local(states, targets, start_coef, washout):
    f32, bf16 = jnp.float32, jnp.bfloat16
    vmem = pl.BlockSpec(memory_space=pltpu.VMEM)
    hbm = pl.BlockSpec(memory_space=pltpu.HBM)
    out = jax.ShapeDtypeStruct((OUT, SAMP), f32)
    dma = pltpu.SemaphoreType.DMA
    return pl.pallas_call(
        kernel,
        out_shape=(out, out),
        in_specs=[hbm] * 4,
        out_specs=(vmem, vmem),
        scratch_shapes=[
            pltpu.VMEM((SAMP, DIM), bf16),
            pltpu.VMEM((2, OUT, SAMP), f32),
            pltpu.VMEM((1, SAMP), jnp.int32),
            pltpu.VMEM((32, SAMP, DIM), bf16),
            pltpu.VMEM((16, SAMP, DIM), bf16),
            pltpu.VMEM((1024, 2048), bf16),
            pltpu.VMEM((1024, 2048), bf16),
            pltpu.VMEM((2048, 256), bf16),
            pltpu.VMEM((1024, 128), f32),
            pltpu.VMEM((128, 128), f32),
            pltpu.VMEM((32, 16, 128), f32),
            pltpu.VMEM((16, 16, 128), f32),
            pltpu.VMEM((16, 16, 128), f32),
            pltpu.VMEM((32, 16, 128), f32),
            pltpu.VMEM((16, 16, 128), f32),
            pltpu.VMEM((16, 16, 128), f32),
            pltpu.VMEM((16, 16, 128), f32),
            pltpu.VMEM((2, 8, 128), f32),
            pltpu.VMEM((32, 8, 128), f32),
            pltpu.VMEM((16, 8, 128), f32),
            dma((4,)),
            dma((9,)),
            dma((3,)),
            dma((16,)),
            dma((8,)),
            dma((16,)),
            dma((16,)),
            dma((8,)),
            dma((10,)),
        ],
        compiler_params=pltpu.CompilerParams(
            collective_id=0, has_side_effects=True, vmem_limit_bytes=48 * 1024 * 1024
        ),
    )(states, targets, start_coef, washout.reshape(1, SAMP))


def solution(mesh):
    return jax.shard_map(
        local,
        mesh=mesh,
        in_specs=(
            P(("row", "col"), None),
            P(None, ("row", "col")),
            P(None, ("row", "col")),
            P(("row", "col")),
        ),
        out_specs=(P(None, ("row", "col")), P(None, ("row", "col"))),
        check_vma=False,
    )
```

```python
import math

import jax
import jax.numpy as jnp
from jax import lax
from jax.experimental import pallas as pl
from jax.experimental.pallas import tpu as pltpu
from jax.sharding import PartitionSpec as P

MESH = pl.DeviceIdType.MESH
RING = 8
SAMP = 64
DIM = 512
OUT = 32
SLOTS = [
    (0, 0), (0, 1), (-2, 0), (2, 0),
    (-1, 0), (1, 0), (-2, 1), (2, 1),
    (-3, 0), (3, 0), (-1, 1), (1, 1),
    (-3, 1), (3, 1), (4, 0), (4, 1),
]
INDEX = {slot: at for at, slot in enumerate(SLOTS)}
GROUPS = [(0, 4), (4, 4), (8, 4), (12, 2), (14, 2)]
EXP_SCALE = math.log2(math.e) * 2.0 / DIM


def place(d, a):
    return INDEX[(d + RING // 2 - 1) % RING - RING // 2 + 1, a % 2]


def mirror(s):
    return place(-SLOTS[s][0], SLOTS[s][1])


def far_first(pair_hops):
    return sorted(range(1, 16), key=lambda s: -abs(SLOTS[s][0]) - pair_hops * SLOTS[s][1])


def lane_group():
    return lax.broadcasted_iota(jnp.int32, (16, 128), 1) // OUT


def by_group(pieces):
    group = lane_group()
    out = pieces[3]
    for g in (2, 1, 0):
        out = jnp.where(group == g, pieces[g], out)
    return out


def pack(block, at):
    return by_group(
        [
            pltpu.roll(block[16 * g : 16 * g + 16], (OUT * (g - at)) % 128, axis=1)
            if g != at
            else block[16 * g : 16 * g + 16]
            for g in range(4)
        ]
    )


def fold_lanes(x):
    x = x + pltpu.roll(x, 64, axis=1)
    return x + pltpu.roll(x, 32, axis=1)


def kernel(
    states_in, targets_in, coef_in, washout_in,
    coef_out, res_out,
    states, vectors, washout, col_st, row_st, e_hi, e_lo, w_all, acc, flip,
    vec0, part1, got1, vec1, vec1r, part2, got2, dots, got_dots, got_dots2,
    in_sem, send_sem, sib_send, c_recv, s_recv, r_recv, v_recv, vs_recv, phase_recv,
):
    row, col = lax.axis_index("row"), lax.axis_index("col")
    core, xl, y = row % 2, (row // 2) % 2, row // 4
    xh, z = col % 2, col // 2

    def row_peer(dy, dxl, dcore):
        return (((y + dy + RING) % RING * 2 + (xl + dxl) % 2) * 2 + (core + dcore) % 2, col)

    def col_peer(dz, dxh):
        return (row, (z + dz + RING) % RING * 2 + (xh + dxh) % 2)

    sibling = row_peer(0, 0, 1)
    near = [row_peer(1, 0, 0), row_peer(-1, 0, 0), row_peer(0, 1, 0), sibling]
    near += [col_peer(1, 0), col_peer(-1, 0), col_peer(0, 1)]
    near += [row_peer(2, 0, 0), row_peer(-2, 0, 0), col_peer(2, 0), col_peer(-2, 0)]

    barrier = pltpu.get_barrier_semaphore()
    for who in near:
        pl.semaphore_signal(barrier, inc=1, device_id=who, device_id_type=MESH)

    fetches = [
        pltpu.make_async_copy(states_in, states, in_sem.at[0]),
        pltpu.make_async_copy(targets_in, vectors.at[0], in_sem.at[1]),
        pltpu.make_async_copy(coef_in, vectors.at[1], in_sem.at[2]),
        pltpu.make_async_copy(washout_in, washout, in_sem.at[3]),
    ]
    for fetch in fetches:
        fetch.start()
    fetches[0].wait()
    pl.semaphore_wait(barrier, len(near))

    def send(src, dst, to, s_sem, r_sem):
        pltpu.make_async_remote_copy(
            src_ref=src, dst_ref=dst, send_sem=s_sem, recv_sem=r_sem, device_id=to, device_id_type=MESH
        ).start()

    def wait(ref, sem):
        pltpu.make_async_copy(ref, ref, sem).wait()

    def hop(s, d, a=0, half=None):
        to = place(SLOTS[s][0] - d, SLOTS[s][1] + a)
        rows = pl.ds(0, SAMP) if half is None else pl.ds(half * 32, 32)
        sem = to if half is None or half == 0 else 16 + SLOTS[to][1]
        for buf, peer, k, recv in ((row_st, col_peer(d, a), 1, r_recv), (col_st, row_peer(d, a, 0), 0, c_recv)):
            src = buf.at[s, rows] if s else states
            send(src, buf.at[to, rows], peer, send_sem.at[k], recv.at[sem])

    def hop_vector(s, d, a=0):
        to = place(SLOTS[s][0] - d, SLOTS[s][1] + a)
        send(vec0.at[s], vec0.at[to], row_peer(d, a, 0), send_sem.at[2], v_recv.at[to])

    def take(s):
        for buf, recv in ((row_st, r_recv), (col_st, c_recv)):
            if SLOTS[s][0] == 4:
                wait(buf.at[s, pl.ds(0, 32)], recv.at[s])
                wait(buf.at[s, pl.ds(32, 32)], recv.at[16 + SLOTS[s][1]])
            else:
                wait(buf.at[s], recv.at[s])

    def take_vector(s):
        wait(vec0.at[s], v_recv.at[s])

    def share(g):
        first, count = GROUPS[g]
        own, other = pl.ds(first, count), pl.ds(16 + first, count)
        send(col_st.at[own], col_st.at[other], sibling, sib_send.at[0], s_recv.at[g])
        send(vec0.at[own], vec0.at[other], sibling, sib_send.at[1], vs_recv.at[g])

    hop(0, 0, 1)
    hop(0, 2)
    hop(0, -2)
    col_st[0] = states[...]
    row_st[0] = states[...]

    own_f = states[...].astype(jnp.float32)
    norm = jnp.sum(own_f * own_f, axis=1, keepdims=True)
    damp_col = jnp.broadcast_to(jnp.exp(norm * (-1.0 / DIM)), (SAMP, 128))
    damp = by_group([damp_col[16 * g : 16 * g + 16] for g in range(4)])
    for fetch in fetches[1:]:
        fetch.wait()
    flip[0:OUT, 0:SAMP] = vectors[0]
    flip[OUT : 2 * OUT, 0:SAMP] = vectors[1]
    flip[2 * OUT : 3 * OUT, 0:SAMP] = jnp.broadcast_to(washout[...].astype(jnp.float32), (OUT, SAMP))
    turned = flip[...].T[0:SAMP]
    mask = pack(turned, 2)
    target = pack(turned, 0) * mask
    start = pack(turned, 1)
    scale = mask * damp
    vec0[0] = scale * start

    hop_vector(0, 0, 1)
    hop_vector(0, 2)
    hop_vector(0, -2)

    group = lane_group()

    def spread(vec, first, count):
        for s in range(first, first + count):
            v = vec[s]
            hi = v.astype(jnp.bfloat16).astype(jnp.float32)
            lo = v - hi
            for g in range(4):
                keep = group == g
                at = SAMP * s + 16 * g
                w_all[at : at + 16, 0:128] = jnp.where(keep, hi, 0.0).astype(jnp.bfloat16)
                w_all[at : at + 16, 128:256] = jnp.where(keep, lo, 0.0).astype(jnp.bfloat16)

    def product(hi, lo, w):
        both = jnp.dot(hi, w, preferred_element_type=jnp.float32)
        low = jnp.dot(lo, w[:, 0:128], preferred_element_type=jnp.float32)
        return both[:, 0:128] + both[:, 128:256] + low

    def tile(r_first, r_count, ranges, fresh):
        left = row_st[r_first : r_first + r_count].reshape(r_count * SAMP, DIM)
        right = jnp.concatenate([col_st[a : a + k].reshape(k * SAMP, DIM) for a, k in ranges], axis=0)
        w = jnp.concatenate([w_all[a * SAMP : (a + k) * SAMP] for a, k in ranges], axis=0)
        cross = lax.dot_general(left, right, (((1,), (1,)), ((), ())), preferred_element_type=jnp.float32)
        e = jnp.exp2(cross * EXP_SCALE)
        hi = e.astype(jnp.bfloat16)
        lo = (e - hi.astype(jnp.float32)).astype(jnp.bfloat16)
        rows = pl.ds(r_first * SAMP, r_count * SAMP)
        at = 0
        for a, k in ranges:
            columns = pl.ds(a * SAMP, k * SAMP)
            e_hi[rows, columns] = hi[:, at : at + k * SAMP]
            e_lo[rows, columns] = lo[:, at : at + k * SAMP]
            at += k * SAMP
        add = product(hi, lo, w)
        acc[rows, :] = add if fresh else acc[rows, :] + add

    def compute(g):
        first, count = GROUPS[g]
        spread(vec0, first, count)
        if first:
            tile(first, count, [(0, first), (16, first)], True)
        tile(0, first + count, [(first, count)], first == 0)
        wait(col_st.at[pl.ds(16 + first, count)], s_recv.at[g])
        wait(vec0.at[pl.ds(16 + first, count)], vs_recv.at[g])
        spread(vec0, 16 + first, count)
        tile(0, first + count, [(16 + first, count)], False)

    sides = (-1, 1)
    pair = place(0, 1)
    take(pair)
    for side in sides:
        hop(pair, 2 * side)
    for side in sides:
        hop(0, side)
    take_vector(pair)
    for side in sides:
        hop_vector(pair, 2 * side)
        hop_vector(0, side)
    for side in sides:
        take(place(2 * side, 0))
        hop(place(2 * side, 0), -side)
    for side in sides:
        take_vector(place(2 * side, 0))
        hop_vector(place(2 * side, 0), -side)
    share(0)
    compute(0)
    for side in sides:
        take(place(2 * side, 1))
        hop(place(2 * side, 1), -side)
    for side in sides:
        hop(pair, side)
    for side in sides:
        take_vector(place(2 * side, 1))
        hop_vector(place(2 * side, 1), -side)
        hop_vector(pair, side)
    for side in sides:
        take(place(side, 0))
        take_vector(place(side, 0))
    share(1)
    for side in sides:
        take(place(3 * side, 0))
        hop(place(3 * side, 0), -side, half=(side + 1) // 2)
    for side in sides:
        take_vector(place(3 * side, 0))
    hop_vector(place(-3, 0), 1)
    compute(1)
    for side in sides:
        take(place(3 * side, 1))
        hop(place(3 * side, 1), -side, half=(side + 1) // 2)
    for side in sides:
        take_vector(place(3 * side, 1))
    hop_vector(place(3, 1), -1)
    share(3)
    for side in sides:
        take(place(side, 1))
        take_vector(place(side, 1))
    share(2)
    compute(2)
    compute(3)
    for a in (0, 1):
        take(place(4, a))
        take_vector(place(4, a))
    share(4)
    compute(4)

    row_far, col_far = far_first(1), far_first(2)

    def to_owner(part, got, s, s_sem, r_sem):
        whole = fold_lanes(acc[SAMP * s : SAMP * s + SAMP, :])
        part[s] = by_group([whole[16 * g : 16 * g + 16] for g in range(4)])
        if s:
            send(part.at[s], got.at[mirror(s)], col_peer(*SLOTS[s]), s_sem, r_sem)

    for s in col_far + [0]:
        to_owner(part1, got1, s, send_sem.at[3], phase_recv.at[0])
    wait(got1.at[pl.ds(1, 15)], phase_recv.at[0])
    total = part1[0]
    for s in range(1, 16):
        total = total + got1[s]
    r0 = target - (scale * total + start)
    weight = scale * r0
    vec1[0] = weight
    vec1r[0] = weight

    for s in row_far:
        at = mirror(s)
        send(vec1.at[0], vec1.at[at], row_peer(*SLOTS[s], 0), send_sem.at[4], phase_recv.at[1 if at < 8 else 2])
    send(vec1.at[0], vec1.at[16], sibling, sib_send.at[2], phase_recv.at[3])
    for s in col_far:
        send(vec1r.at[0], vec1r.at[mirror(s)], col_peer(*SLOTS[s]), send_sem.at[5], phase_recv.at[6])

    def second(first, count, fresh, rows):
        columns = pl.ds(first * SAMP, count * SAMP)
        add = product(e_hi[rows, columns], e_lo[rows, columns], w_all[columns, :])
        acc[rows, :] = add if fresh else acc[rows, :] + add

    every = pl.ds(0, 1024)
    wait(vec1.at[pl.ds(1, 7)], phase_recv.at[1])
    send(vec1.at[pl.ds(1, 7)], vec1.at[pl.ds(17, 7)], sibling, sib_send.at[2], phase_recv.at[4])
    spread(vec1, 0, 8)
    second(0, 8, True, every)
    wait(vec1.at[pl.ds(8, 8)], phase_recv.at[2])
    send(vec1.at[pl.ds(8, 8)], vec1.at[pl.ds(24, 8)], sibling, sib_send.at[2], phase_recv.at[5])
    spread(vec1, 8, 8)
    second(8, 8, False, every)
    wait(vec1.at[16], phase_recv.at[3])
    wait(vec1.at[pl.ds(17, 7)], phase_recv.at[4])
    spread(vec1, 16, 8)
    second(16, 8, False, every)
    wait(vec1.at[pl.ds(24, 8)], phase_recv.at[5])
    spread(vec1, 24, 8)
    for chunk in (3, 2, 1, 0):
        second(24, 8, False, pl.ds(256 * chunk, 256))
        for s in range(4 * chunk + 3, 4 * chunk - 1, -1):
            to_owner(part2, got2, s, send_sem.at[6], phase_recv.at[7])

    wait(vec1r.at[pl.ds(1, 15)], phase_recv.at[6])
    bend = vec1r[0] * part2[0]
    for s in range(1, 16):
        bend = bend + vec1r[s] * part2[s]
    bend = jnp.sum(bend, axis=0, keepdims=True)
    squares = jnp.sum(r0 * r0, axis=0, keepdims=True)
    first_row = lax.broadcasted_iota(jnp.int32, (8, 128), 0) == 0
    both = fold_lanes(jnp.where(first_row, jnp.broadcast_to(bend, (8, 128)), jnp.broadcast_to(squares, (8, 128))))
    dots[0] = both
    two = pl.ds(0, 2)
    for s in row_far + [0]:
        for dcore in (1, 0):
            if s or dcore:
                at = 16 * dcore + mirror(s)
                to = row_peer(*SLOTS[s], dcore)
                send(dots.at[0, two], got_dots.at[at, two], to, send_sem.at[7], phase_recv.at[8])
    wait(got_dots.at[pl.ds(1, 31), two], phase_recv.at[8])
    both = both[0:2]
    for s in range(1, 32):
        both = both + got_dots[s, 0:2, :]
    dots[1, 0:2, :] = both
    for s in col_far:
        to = col_peer(*SLOTS[s])
        send(dots.at[1, two], got_dots2.at[mirror(s), two], to, send_sem.at[8], phase_recv.at[9])
    wait(got2.at[pl.ds(1, 15)], phase_recv.at[7])
    total = part2[0]
    for s in range(1, 16):
        total = total + got2[s]
    q = scale * total + r0
    wait(got_dots2.at[pl.ds(1, 15), two], phase_recv.at[9])
    for s in range(1, 16):
        both = both + got_dots2[s, 0:2, :]
    squares = both[1:2]
    alpha = squares / (both[0:1] + squares)
    coef = start + alpha * r0
    res = r0 - alpha * q
    low = lax.broadcasted_iota(jnp.int32, (16, 128), 1) < OUT
    for g in range(4):
        a = pltpu.roll(coef, (128 - OUT * g) % 128, axis=1) if g else coef
        b = pltpu.roll(res, (128 + OUT - OUT * g) % 128, axis=1) if g != 1 else res
        flip[16 * g : 16 * g + 16, :] = jnp.where(low, a, b)
    back = flip[...].T
    coef_out[...] = back[0:OUT, 0:SAMP]
    res_out[...] = back[OUT : 2 * OUT, 0:SAMP]

    wait(col_st.at[pl.ds(0, 15)], send_sem.at[0])
    wait(row_st.at[pl.ds(0, 15)], send_sem.at[1])
    wait(vec0.at[pl.ds(0, 15)], send_sem.at[2])
    wait(col_st.at[pl.ds(0, 16)], sib_send.at[0])
    wait(vec0.at[pl.ds(0, 16)], sib_send.at[1])
    wait(vec1.at[pl.ds(0, 16)], sib_send.at[2])
    wait(part1.at[pl.ds(0, 15)], send_sem.at[3])
    wait(vec1.at[pl.ds(0, 15)], send_sem.at[4])
    wait(vec1r.at[pl.ds(0, 15)], send_sem.at[5])
    wait(part2.at[pl.ds(0, 15)], send_sem.at[6])
    wait(got_dots.at[pl.ds(0, 31), two], send_sem.at[7])
    wait(got_dots2.at[pl.ds(0, 15), two], send_sem.at[8])


def local(states, targets, start_coef, washout):
    f32, bf16 = jnp.float32, jnp.bfloat16
    vmem = pl.BlockSpec(memory_space=pltpu.VMEM)
    hbm = pl.BlockSpec(memory_space=pltpu.HBM)
    out = jax.ShapeDtypeStruct((OUT, SAMP), f32)
    dma = pltpu.SemaphoreType.DMA
    return pl.pallas_call(
        kernel,
        out_shape=(out, out),
        in_specs=[hbm] * 4,
        out_specs=(vmem, vmem),
        scratch_shapes=[
            pltpu.VMEM((SAMP, DIM), bf16),
            pltpu.VMEM((2, OUT, SAMP), f32),
            pltpu.VMEM((1, SAMP), jnp.int32),
            pltpu.VMEM((32, SAMP, DIM), bf16),
            pltpu.VMEM((16, SAMP, DIM), bf16),
            pltpu.VMEM((1024, 2048), bf16),
            pltpu.VMEM((1024, 2048), bf16),
            pltpu.VMEM((2048, 256), bf16),
            pltpu.VMEM((1024, 128), f32),
            pltpu.VMEM((128, 128), f32),
            pltpu.VMEM((32, 16, 128), f32),
            pltpu.VMEM((16, 16, 128), f32),
            pltpu.VMEM((16, 16, 128), f32),
            pltpu.VMEM((32, 16, 128), f32),
            pltpu.VMEM((16, 16, 128), f32),
            pltpu.VMEM((16, 16, 128), f32),
            pltpu.VMEM((16, 16, 128), f32),
            pltpu.VMEM((2, 8, 128), f32),
            pltpu.VMEM((32, 8, 128), f32),
            pltpu.VMEM((16, 8, 128), f32),
            dma((4,)),
            dma((9,)),
            dma((3,)),
            dma((18,)),
            dma((5,)),
            dma((18,)),
            dma((16,)),
            dma((5,)),
            dma((10,)),
        ],
        compiler_params=pltpu.CompilerParams(
            collective_id=0, has_side_effects=True, vmem_limit_bytes=60 * 1024 * 1024
        ),
    )(states, targets, start_coef, washout.reshape(1, SAMP))


def solution(mesh):
    return jax.shard_map(
        local,
        mesh=mesh,
        in_specs=(
            P(("row", "col"), None),
            P(None, ("row", "col")),
            P(None, ("row", "col")),
            P(("row", "col")),
        ),
        out_specs=(P(None, ("row", "col")), P(None, ("row", "col"))),
        check_vma=False,
    )
```

```python
import math

import jax
import jax.numpy as jnp
from jax import lax
from jax.experimental import pallas as pl
from jax.experimental.pallas import tpu as pltpu
from jax.sharding import PartitionSpec as P

MESH = pl.DeviceIdType.MESH
RING = 8
SAMP = 64
DIM = 512
OUT = 32
SLOTS = [
    (0, 0), (0, 1), (-2, 0), (2, 0),
    (-1, 0), (1, 0), (-2, 1), (2, 1), (-3, 0), (3, 0),
    (-1, 1), (1, 1), (-3, 1), (3, 1),
    (4, 0), (4, 1),
]
INDEX = {slot: at for at, slot in enumerate(SLOTS)}
GROUPS = [(0, 4), (4, 6), (10, 4)]
SOONER = 14
EXP_SCALE = math.log2(math.e) * 2.0 / DIM


def place(d, a):
    return INDEX[(d + RING // 2 - 1) % RING - RING // 2 + 1, a % 2]


def mirror(s):
    return place(-SLOTS[s][0], SLOTS[s][1])


def far_first(pair_hops):
    return sorted(range(1, 16), key=lambda s: -abs(SLOTS[s][0]) - pair_hops * SLOTS[s][1])


def lane_group():
    return lax.broadcasted_iota(jnp.int32, (16, 128), 1) // OUT


def by_group(pieces):
    group = lane_group()
    out = pieces[3]
    for g in (2, 1, 0):
        out = jnp.where(group == g, pieces[g], out)
    return out


def pack(block, at):
    return by_group(
        [
            pltpu.roll(block[16 * g : 16 * g + 16], (OUT * (g - at)) % 128, axis=1)
            if g != at
            else block[16 * g : 16 * g + 16]
            for g in range(4)
        ]
    )


def fold_lanes(x):
    x = x + pltpu.roll(x, 64, axis=1)
    return x + pltpu.roll(x, 32, axis=1)


def kernel(
    states_in, targets_in, coef_in, washout_in,
    both_out,
    states, vectors, washout, col_st, row_st, e_hi, e_lo, w_all, acc, flip,
    vec0, part1, got1, vec1, vec1r, part2, got2, dots, got_dots, got_dots2,
    in_sem, send_sem, sib_send, c_recv, s_recv, r_recv, v_recv, vs_recv, phase_recv,
):
    row, col = lax.axis_index("row"), lax.axis_index("col")
    core, xl, y = row % 2, (row // 2) % 2, row // 4
    xh, z = col % 2, col // 2

    def row_peer(dy, dxl, dcore):
        return (((y + dy + RING) % RING * 2 + (xl + dxl) % 2) * 2 + (core + dcore) % 2, col)

    def col_peer(dz, dxh):
        return (row, (z + dz + RING) % RING * 2 + (xh + dxh) % 2)

    sibling = row_peer(0, 0, 1)
    near = [row_peer(1, 0, 0), row_peer(-1, 0, 0), row_peer(0, 1, 0), sibling]
    near += [col_peer(1, 0), col_peer(-1, 0), col_peer(0, 1)]
    near += [row_peer(2, 0, 0), row_peer(-2, 0, 0), col_peer(2, 0), col_peer(-2, 0)]

    barrier = pltpu.get_barrier_semaphore()
    for who in near:
        pl.semaphore_signal(barrier, inc=1, device_id=who, device_id_type=MESH)

    fetches = [
        pltpu.make_async_copy(states_in, states, in_sem.at[0]),
        pltpu.make_async_copy(targets_in, vectors.at[0], in_sem.at[1]),
        pltpu.make_async_copy(coef_in, vectors.at[1], in_sem.at[2]),
        pltpu.make_async_copy(washout_in, washout, in_sem.at[3]),
    ]
    for fetch in fetches:
        fetch.start()
    fetches[0].wait()
    pl.semaphore_wait(barrier, len(near))

    def send(src, dst, to, s_sem, r_sem):
        pltpu.make_async_remote_copy(
            src_ref=src, dst_ref=dst, send_sem=s_sem, recv_sem=r_sem, device_id=to, device_id_type=MESH
        ).start()

    def wait(ref, sem):
        pltpu.make_async_copy(ref, ref, sem).wait()

    def hop(s, d, a=0, half=None):
        to = place(SLOTS[s][0] - d, SLOTS[s][1] + a)
        rows = pl.ds(0, SAMP) if half is None else pl.ds(half * 32, 32)
        sem = to if half is None or half == 0 else 16 + SLOTS[to][1]
        for buf, peer, k, recv in ((row_st, col_peer(d, a), 1, r_recv), (col_st, row_peer(d, a, 0), 0, c_recv)):
            src = buf.at[s, rows] if s else states
            send(src, buf.at[to, rows], peer, send_sem.at[k], recv.at[sem])
        if half is not None:
            both = s_recv.at[4 + 2 * half + SLOTS[to][1]]
            send(col_st.at[s, rows], col_st.at[16 + to, rows], row_peer(d, a, 1), send_sem.at[0], both)

    def hop_vector(s, d, a=0):
        to = place(SLOTS[s][0] - d, SLOTS[s][1] + a)
        send(vec0.at[s], vec0.at[to], row_peer(d, a, 0), send_sem.at[2], v_recv.at[to])
        if SLOTS[to][0] == 4:
            both = vs_recv.at[1 + SLOTS[to][1]]
            send(vec0.at[s], vec0.at[16 + to], row_peer(d, a, 1), send_sem.at[2], both)

    def take(s):
        for buf, recv in ((row_st, r_recv), (col_st, c_recv)):
            if SLOTS[s][0] == 4:
                wait(buf.at[s, pl.ds(0, 32)], recv.at[s])
                wait(buf.at[s, pl.ds(32, 32)], recv.at[16 + SLOTS[s][1]])
            else:
                wait(buf.at[s], recv.at[s])
        if SLOTS[s][0] == 4:
            for half in (0, 1):
                wait(col_st.at[16 + s, pl.ds(32 * half, 32)], s_recv.at[4 + 2 * half + SLOTS[s][1]])

    def take_vector(s):
        wait(vec0.at[s], v_recv.at[s])
        if SLOTS[s][0] == 4:
            wait(vec0.at[16 + s], vs_recv.at[1 + SLOTS[s][1]])

    def share(g):
        first, count = GROUPS[g]
        own, other = pl.ds(first, count), pl.ds(16 + first, count)
        send(col_st.at[own], col_st.at[other], sibling, sib_send.at[0], s_recv.at[g])

    hop(0, 0, 1)
    hop(0, 2)
    hop(0, -2)
    col_st[0] = states[...]
    row_st[0] = states[...]

    own_f = states[...].astype(jnp.float32)
    norm = jnp.sum(own_f * own_f, axis=1, keepdims=True)
    damp_col = jnp.broadcast_to(jnp.exp(norm * (-1.0 / DIM)), (SAMP, 128))
    damp = by_group([damp_col[16 * g : 16 * g + 16] for g in range(4)])
    for fetch in fetches[1:]:
        fetch.wait()
    flip[0:OUT, 0:SAMP] = vectors[0]
    flip[OUT : 2 * OUT, 0:SAMP] = vectors[1]
    flip[2 * OUT : 3 * OUT, 0:SAMP] = jnp.broadcast_to(washout[...].astype(jnp.float32), (OUT, SAMP))
    turned = flip[...].T[0:SAMP]
    mask = pack(turned, 2)
    target = pack(turned, 0) * mask
    start = pack(turned, 1)
    scale = mask * damp
    vec0[0] = scale * start

    hop_vector(0, 0, 1)
    hop_vector(0, 2)
    hop_vector(0, -2)

    group = lane_group()

    def spread(vec, first, count):
        for s in range(first, first + count):
            v = vec[s]
            hi = v.astype(jnp.bfloat16).astype(jnp.float32)
            lo = v - hi
            for g in range(4):
                keep = group == g
                at = SAMP * s + 16 * g
                w_all[at : at + 16, 0:128] = jnp.where(keep, hi, 0.0).astype(jnp.bfloat16)
                w_all[at : at + 16, 128:256] = jnp.where(keep, lo, 0.0).astype(jnp.bfloat16)

    def product(rows, ranges):
        columns = [pl.ds(a * SAMP, k * SAMP) for a, k in ranges]
        hi, lo = [jnp.concatenate([e[rows, c] for c in columns], axis=1) for e in (e_hi, e_lo)]
        w = jnp.concatenate([w_all[c, :] for c in columns], axis=0)
        both = jnp.dot(hi, w, preferred_element_type=jnp.float32)
        low = jnp.dot(lo, w[:, 0:128], preferred_element_type=jnp.float32)
        return both[:, 0:128] + both[:, 128:256] + low

    def tile(r_first, r_count, ranges):
        left = row_st[r_first : r_first + r_count].reshape(r_count * SAMP, DIM)
        right = jnp.concatenate([col_st[a : a + k].reshape(k * SAMP, DIM) for a, k in ranges], axis=0)
        cross = lax.dot_general(left, right, (((1,), (1,)), ((), ())), preferred_element_type=jnp.float32)
        e = jnp.exp2(cross * EXP_SCALE)
        hi = e.astype(jnp.bfloat16)
        lo = (e - hi.astype(jnp.float32)).astype(jnp.bfloat16)
        rows = pl.ds(r_first * SAMP, r_count * SAMP)
        at = 0
        for a, k in ranges:
            columns = pl.ds(a * SAMP, k * SAMP)
            e_hi[rows, columns] = hi[:, at : at + k * SAMP]
            e_lo[rows, columns] = lo[:, at : at + k * SAMP]
            at += k * SAMP

    def grow(g):
        first, count = GROUPS[g]
        if first:
            tile(first, count, [(0, first), (16, first)])
        tile(0, first + count, [(first, count)])
        wait(col_st.at[pl.ds(16 + first, count)], s_recv.at[g])
        tile(0, first + count, [(16 + first, count)])

    sides = (-1, 1)
    pair = place(0, 1)
    take(pair)
    for side in sides:
        hop(pair, 2 * side)
    for side in sides:
        hop(0, side)
    for side in sides:
        take(place(2 * side, 0))
        hop(place(2 * side, 0), -side)
    share(0)
    take_vector(pair)
    for side in sides:
        hop_vector(pair, 2 * side)
        hop_vector(0, side)
    for side in sides:
        take_vector(place(2 * side, 0))
        hop_vector(place(2 * side, 0), -side)
    grow(0)
    for side in sides:
        take(place(2 * side, 1))
        hop(place(2 * side, 1), -side)
    for side in sides:
        hop(pair, side)
    for side in sides:
        take(place(side, 0))
    for side in sides:
        take(place(3 * side, 0))
        hop(place(3 * side, 0), -side, half=(side + 1) // 2)
    share(1)
    for side in sides:
        take_vector(place(2 * side, 1))
        hop_vector(place(2 * side, 1), -side)
        hop_vector(pair, side)
        take_vector(place(side, 0))
    for side in sides:
        take_vector(place(3 * side, 0))
    hop_vector(place(-3, 0), 1)
    grow(1)
    for side in sides:
        take(place(3 * side, 1))
        hop(place(3 * side, 1), -side, half=(side + 1) // 2)
    for side in sides:
        take(place(side, 1))
    share(2)
    for side in sides:
        take_vector(place(3 * side, 1))
        take_vector(place(side, 1))
    hop_vector(place(3, 1), -1)
    sooner, shared = pl.ds(0, SOONER), pl.ds(16, SOONER)
    send(vec0.at[sooner], vec0.at[shared], sibling, sib_send.at[1], vs_recv.at[0])
    grow(2)
    wait(vec0.at[shared], vs_recv.at[0])
    spread(vec0, 0, SOONER)
    spread(vec0, 16, SOONER)
    for first, count in ((0, 256), (256, 256), (512, 256), (768, 128)):
        rows = pl.ds(first, count)
        acc[rows, :] = product(rows, [(0, SOONER), (16, SOONER)])
    for a in (0, 1):
        take(place(4, a))
        take_vector(place(4, a))

    row_far, col_far = far_first(1), far_first(2)

    def to_owner(part, got, s, s_sem, r_sem):
        whole = fold_lanes(acc[SAMP * s : SAMP * s + SAMP, :])
        part[s] = by_group([whole[16 * g : 16 * g + 16] for g in range(4)])
        if s:
            send(part.at[s], got.at[mirror(s)], col_peer(*SLOTS[s]), s_sem, r_sem)

    last = [(SOONER, 2), (16 + SOONER, 2)]
    spread(vec0, SOONER, 2)
    spread(vec0, 16 + SOONER, 2)
    tile(SOONER, 2, [(0, SOONER), (16, SOONER)])
    for first, count in ((14, 2), (10, 4), (6, 4), (4, 2), (0, 4)):
        rows = pl.ds(first * SAMP, count * SAMP)
        tile(first, count, last)
        if first == SOONER:
            acc[rows, :] = product(rows, [(0, 32)])
        else:
            acc[rows, :] += product(rows, last)
        for s in range(first + count - 1, first - 1, -1):
            to_owner(part1, got1, s, send_sem.at[3], phase_recv.at[0])
    wait(got1.at[pl.ds(1, 15)], phase_recv.at[0])
    total = part1[0]
    for s in range(1, 16):
        total = total + got1[s]
    r0 = target - (scale * total + start)
    weight = scale * r0
    vec1[0] = weight
    vec1r[0] = weight

    for s in row_far:
        at = mirror(s)
        send(vec1.at[0], vec1.at[at], row_peer(*SLOTS[s], 0), send_sem.at[4], phase_recv.at[1 if at < 12 else 2])
    send(vec1.at[0], vec1.at[16], sibling, sib_send.at[2], phase_recv.at[3])
    for s in col_far:
        send(vec1r.at[0], vec1r.at[mirror(s)], col_peer(*SLOTS[s]), send_sem.at[5], phase_recv.at[6])

    def second(first, count, fresh, rows):
        add = product(rows, [(first, count)])
        acc[rows, :] = add if fresh else acc[rows, :] + add

    every = pl.ds(0, 1024)
    wait(vec1.at[pl.ds(1, 11)], phase_recv.at[1])
    send(vec1.at[pl.ds(1, 11)], vec1.at[pl.ds(17, 11)], sibling, sib_send.at[2], phase_recv.at[4])
    spread(vec1, 0, 12)
    second(0, 12, True, every)
    wait(vec1.at[pl.ds(12, 4)], phase_recv.at[2])
    send(vec1.at[pl.ds(12, 4)], vec1.at[pl.ds(28, 4)], sibling, sib_send.at[2], phase_recv.at[5])
    spread(vec1, 12, 4)
    second(12, 4, False, every)
    wait(vec1.at[16], phase_recv.at[3])
    wait(vec1.at[pl.ds(17, 11)], phase_recv.at[4])
    spread(vec1, 16, 12)
    second(16, 12, False, every)
    wait(vec1.at[pl.ds(28, 4)], phase_recv.at[5])
    spread(vec1, 28, 4)
    for chunk in (3, 2, 1, 0):
        second(28, 4, False, pl.ds(256 * chunk, 256))
        for s in range(4 * chunk + 3, 4 * chunk - 1, -1):
            to_owner(part2, got2, s, send_sem.at[6], phase_recv.at[7])

    wait(vec1r.at[pl.ds(1, 15)], phase_recv.at[6])
    bend = vec1r[0] * part2[0]
    for s in range(1, 16):
        bend = bend + vec1r[s] * part2[s]
    bend = jnp.sum(bend, axis=0, keepdims=True)
    squares = jnp.sum(r0 * r0, axis=0, keepdims=True)
    first_row = lax.broadcasted_iota(jnp.int32, (8, 128), 0) == 0
    both = fold_lanes(jnp.where(first_row, jnp.broadcast_to(bend, (8, 128)), jnp.broadcast_to(squares, (8, 128))))
    dots[0] = both
    two = pl.ds(0, 2)
    for s in row_far + [0]:
        for dcore in (1, 0):
            if s or dcore:
                at = 16 * dcore + mirror(s)
                to = row_peer(*SLOTS[s], dcore)
                send(dots.at[0, two], got_dots.at[at, two], to, send_sem.at[7], phase_recv.at[8])
    wait(got_dots.at[pl.ds(1, 31), two], phase_recv.at[8])
    both = both[0:2]
    for s in range(1, 32):
        both = both + got_dots[s, 0:2, :]
    dots[1, 0:2, :] = both
    for s in col_far:
        to = col_peer(*SLOTS[s])
        send(dots.at[1, two], got_dots2.at[mirror(s), two], to, send_sem.at[8], phase_recv.at[9])
    wait(got2.at[pl.ds(1, 15)], phase_recv.at[7])
    total = part2[0]
    for s in range(1, 16):
        total = total + got2[s]
    q = scale * total + r0
    wait(got_dots2.at[pl.ds(1, 15), two], phase_recv.at[9])
    for s in range(1, 16):
        both = both + got_dots2[s, 0:2, :]
    squares = both[1:2]
    alpha = squares / (both[0:1] + squares)
    coef = start + alpha * r0
    res = r0 - alpha * q
    low = lax.broadcasted_iota(jnp.int32, (16, 128), 1) < OUT
    for g in range(4):
        a = pltpu.roll(coef, (128 - OUT * g) % 128, axis=1) if g else coef
        b = pltpu.roll(res, (128 + OUT - OUT * g) % 128, axis=1) if g != 1 else res
        flip[16 * g : 16 * g + 16, :] = jnp.where(low, a, b)
    back = flip[...].T
    both_out[0] = back[0:OUT, 0:SAMP]
    both_out[1] = back[OUT : 2 * OUT, 0:SAMP]

    wait(col_st.at[pl.ds(0, 17)], send_sem.at[0])
    wait(row_st.at[pl.ds(0, 15)], send_sem.at[1])
    wait(vec0.at[pl.ds(0, 17)], send_sem.at[2])
    wait(col_st.at[pl.ds(0, 14)], sib_send.at[0])
    wait(vec0.at[pl.ds(0, 14)], sib_send.at[1])
    wait(vec1.at[pl.ds(0, 16)], sib_send.at[2])
    wait(part1.at[pl.ds(0, 15)], send_sem.at[3])
    wait(vec1.at[pl.ds(0, 15)], send_sem.at[4])
    wait(vec1r.at[pl.ds(0, 15)], send_sem.at[5])
    wait(part2.at[pl.ds(0, 15)], send_sem.at[6])
    wait(got_dots.at[pl.ds(0, 31), two], send_sem.at[7])
    wait(got_dots2.at[pl.ds(0, 15), two], send_sem.at[8])


def store(both, coef_out, res_out, sem):
    copies = [pltpu.make_async_copy(both.at[k], out, sem.at[k]) for k, out in enumerate((coef_out, res_out))]
    for copy in copies:
        copy.start()
    for copy in copies:
        copy.wait()


def local(states, targets, start_coef, washout):
    f32, bf16 = jnp.float32, jnp.bfloat16
    vmem = pl.BlockSpec(memory_space=pltpu.VMEM)
    hbm = pl.BlockSpec(memory_space=pltpu.HBM)
    dma = pltpu.SemaphoreType.DMA
    inputs = (states, targets, start_coef, washout.reshape(1, SAMP))
    both = pl.pallas_call(
        kernel,
        out_shape=pltpu.VMEM((2, OUT, SAMP), f32),
        in_specs=[hbm] * 4,
        out_specs=vmem,
        scratch_shapes=[
            pltpu.VMEM((SAMP, DIM), bf16),
            pltpu.VMEM((2, OUT, SAMP), f32),
            pltpu.VMEM((1, SAMP), jnp.int32),
            pltpu.VMEM((32, SAMP, DIM), bf16),
            pltpu.VMEM((16, SAMP, DIM), bf16),
            pltpu.VMEM((1024, 2048), bf16),
            pltpu.VMEM((1024, 2048), bf16),
            pltpu.VMEM((2048, 256), bf16),
            pltpu.VMEM((1024, 128), f32),
            pltpu.VMEM((128, 128), f32),
            pltpu.VMEM((32, 16, 128), f32),
            pltpu.VMEM((16, 16, 128), f32),
            pltpu.VMEM((16, 16, 128), f32),
            pltpu.VMEM((32, 16, 128), f32),
            pltpu.VMEM((16, 16, 128), f32),
            pltpu.VMEM((16, 16, 128), f32),
            pltpu.VMEM((16, 16, 128), f32),
            pltpu.VMEM((2, 8, 128), f32),
            pltpu.VMEM((32, 8, 128), f32),
            pltpu.VMEM((16, 8, 128), f32),
            dma((4,)),
            dma((9,)),
            dma((3,)),
            dma((18,)),
            dma((8,)),
            dma((18,)),
            dma((16,)),
            dma((6,)),
            dma((10,)),
        ],
        compiler_params=pltpu.CompilerParams(
            collective_id=0, has_side_effects=True, vmem_limit_bytes=48 * 1024 * 1024
        ),
    )(*[pltpu.with_memory_space_constraint(x, pltpu.HBM) for x in inputs])
    out = jax.ShapeDtypeStruct((OUT, SAMP), f32)
    return pl.pallas_call(
        store,
        out_shape=(out, out),
        in_specs=[vmem],
        out_specs=(hbm, hbm),
        scratch_shapes=[dma((2,))],
    )(both)


def solution(mesh):
    return jax.shard_map(
        local,
        mesh=mesh,
        in_specs=(
            P(("row", "col"), None),
            P(None, ("row", "col")),
            P(None, ("row", "col")),
            P(("row", "col")),
        ),
        out_specs=(P(None, ("row", "col")), P(None, ("row", "col"))),
        check_vma=False,
    )
```

```python
import math

import jax
import jax.numpy as jnp
from jax import lax
from jax.experimental import pallas as pl
from jax.experimental.pallas import tpu as pltpu
from jax.sharding import PartitionSpec as P

MESH = pl.DeviceIdType.MESH
RING = 8
SAMP = 64
DIM = 512
OUT = 32
SLOTS = [
    (0, 0), (0, 1), (-2, 0), (2, 0),
    (-1, 0), (1, 0), (-2, 1), (2, 1), (-3, 0), (3, 0),
    (-1, 1), (1, 1), (-3, 1), (3, 1),
    (4, 0), (4, 1),
]
INDEX = {slot: at for at, slot in enumerate(SLOTS)}
GROUPS = [(0, 4), (4, 6), (10, 4)]
SOONER = 14
ROW_SLOT = 4 * SAMP
COL_SLOT = ROW_SLOT + 32
EXP_SCALE = math.log2(math.e) * 2.0 / DIM


def place(d, a):
    return INDEX[(d + RING // 2 - 1) % RING - RING // 2 + 1, a % 2]


def mirror(s):
    return place(-SLOTS[s][0], SLOTS[s][1])


def far_first(pair_hops):
    return sorted(range(1, 16), key=lambda s: -abs(SLOTS[s][0]) - pair_hops * SLOTS[s][1])


def lane_group():
    return lax.broadcasted_iota(jnp.int32, (16, 128), 1) // OUT


def by_group(pieces):
    group = lane_group()
    out = pieces[3]
    for g in (2, 1, 0):
        out = jnp.where(group == g, pieces[g], out)
    return out


def pack(block, at):
    return by_group(
        [
            pltpu.roll(block[16 * g : 16 * g + 16], (OUT * (g - at)) % 128, axis=1)
            if g != at
            else block[16 * g : 16 * g + 16]
            for g in range(4)
        ]
    )


def fold_lanes(x):
    x = x + pltpu.roll(x, 64, axis=1)
    return x + pltpu.roll(x, 32, axis=1)


def kernel(
    states_in, targets_in, coef_in, washout_in,
    both_out,
    states, vectors, washout, col_st, row_st, e_hi, e_lo, w_all, acc, flip,
    part1, got1, vec1, vec1r, part2, got2, dots, got_dots, got_dots2,
    in_sem, send_sem, sib_send, c_recv, s_recv, r_recv, phase_recv,
):
    row, col = lax.axis_index("row"), lax.axis_index("col")
    core, xl, y = row % 2, (row // 2) % 2, row // 4
    xh, z = col % 2, col // 2

    def row_peer(dy, dxl, dcore):
        return (((y + dy + RING) % RING * 2 + (xl + dxl) % 2) * 2 + (core + dcore) % 2, col)

    def col_peer(dz, dxh):
        return (row, (z + dz + RING) % RING * 2 + (xh + dxh) % 2)

    sibling = row_peer(0, 0, 1)
    near = [row_peer(1, 0, 0), row_peer(-1, 0, 0), row_peer(0, 1, 0), sibling]
    near += [col_peer(1, 0), col_peer(-1, 0), col_peer(0, 1)]
    near += [row_peer(2, 0, 0), row_peer(-2, 0, 0), col_peer(2, 0), col_peer(-2, 0)]

    barrier = pltpu.get_barrier_semaphore()
    for who in near:
        pl.semaphore_signal(barrier, inc=1, device_id=who, device_id_type=MESH)

    fetches = [
        pltpu.make_async_copy(states_in, states, in_sem.at[0]),
        pltpu.make_async_copy(targets_in, vectors.at[0], in_sem.at[1]),
        pltpu.make_async_copy(coef_in, vectors.at[1], in_sem.at[2]),
        pltpu.make_async_copy(washout_in, washout, in_sem.at[3]),
    ]
    for fetch in fetches:
        fetch.start()
    fetches[0].wait()

    def send(src, dst, to, s_sem, r_sem):
        pltpu.make_async_remote_copy(
            src_ref=src, dst_ref=dst, send_sem=s_sem, recv_sem=r_sem, device_id=to, device_id_type=MESH
        ).start()

    def wait(ref, sem):
        pltpu.make_async_copy(ref, ref, sem).wait()

    def send_col(s, d, a=0, half=None):
        to = place(SLOTS[s][0] - d, SLOTS[s][1] + a)
        rows = pl.ds(0, COL_SLOT) if half is None else pl.ds(half * (COL_SLOT // 2), COL_SLOT // 2)
        sem = 16 + SLOTS[to][1] if half else to
        src = col_st.at[s, rows]
        send(src, col_st.at[to, rows], row_peer(d, a, 0), send_sem.at[0], c_recv.at[sem])
        if half is not None:
            both = s_recv.at[4 + 2 * half + SLOTS[to][1]]
            send(src, col_st.at[16 + to, rows], row_peer(d, a, 1), send_sem.at[0], both)

    def send_row(s, d, a=0, half=None):
        to = place(SLOTS[s][0] - d, SLOTS[s][1] + a)
        rows = pl.ds(0, ROW_SLOT) if half is None else pl.ds(half * (ROW_SLOT // 2), ROW_SLOT // 2)
        sem = 16 + SLOTS[to][1] if half else to
        send(row_st.at[s, rows], row_st.at[to, rows], col_peer(d, a), send_sem.at[1], r_recv.at[sem])

    def take_col(s):
        if SLOTS[s][0] == 4:
            for half in (0, 1):
                rows = pl.ds(half * (COL_SLOT // 2), COL_SLOT // 2)
                wait(col_st.at[s, rows], c_recv.at[16 + SLOTS[s][1] if half else s])
                wait(col_st.at[16 + s, rows], s_recv.at[4 + 2 * half + SLOTS[s][1]])
        else:
            wait(col_st.at[s], c_recv.at[s])

    def take_row(s):
        if SLOTS[s][0] == 4:
            for half in (0, 1):
                rows = pl.ds(half * (ROW_SLOT // 2), ROW_SLOT // 2)
                wait(row_st.at[s, rows], r_recv.at[16 + SLOTS[s][1] if half else s])
        else:
            wait(row_st.at[s], r_recv.at[s])

    def share(g):
        first, count = GROUPS[g]
        own, other = pl.ds(first, count), pl.ds(16 + first, count)
        send(col_st.at[own], col_st.at[other], sibling, sib_send.at[0], s_recv.at[g])

    for k in range(4):
        piece = states[:, 128 * k : 128 * k + 128]
        col_st[0, SAMP * k : SAMP * k + SAMP, :] = piece
        row_st[0, SAMP * k : SAMP * k + SAMP, :] = piece
    own_f = states[...].astype(jnp.float32)
    norm = jnp.sum(own_f * own_f, axis=1, keepdims=True)
    damp_col = jnp.broadcast_to(jnp.exp(norm * (-1.0 / DIM)), (SAMP, 128))
    damp = by_group([damp_col[16 * g : 16 * g + 16] for g in range(4)])
    for fetch in fetches[1:]:
        fetch.wait()
    flip[0:OUT, 0:SAMP] = vectors[0]
    flip[OUT : 2 * OUT, 0:SAMP] = vectors[1]
    flip[2 * OUT : 3 * OUT, 0:SAMP] = jnp.broadcast_to(washout[...].astype(jnp.float32), (OUT, SAMP))
    turned = flip[...].T[0:SAMP]
    mask = pack(turned, 2)
    target = pack(turned, 0) * mask
    start = pack(turned, 1)
    scale = mask * damp
    weight = scale * start
    high = weight.astype(jnp.bfloat16)
    col_st[0, ROW_SLOT : ROW_SLOT + 16, :] = high
    col_st[0, ROW_SLOT + 16 : COL_SLOT, :] = (weight - high.astype(jnp.float32)).astype(jnp.bfloat16)
    pl.semaphore_wait(barrier, len(near))

    for way in (send_col, send_row):
        way(0, 0, 1)
        way(0, 2)
        way(0, -2)

    group = lane_group()

    def lay(s, hi, lo):
        for g in range(4):
            keep = group == g
            at = SAMP * s + 16 * g
            w_all[at : at + 16, 0:128] = jnp.where(keep, hi, 0.0).astype(jnp.bfloat16)
            w_all[at : at + 16, 128:256] = jnp.where(keep, lo, 0.0).astype(jnp.bfloat16)

    def spread_sent(first, count):
        for s in range(first, first + count):
            hi = col_st[s, ROW_SLOT : ROW_SLOT + 16, :]
            lo = col_st[s, ROW_SLOT + 16 : COL_SLOT, :]
            lay(s, hi.astype(jnp.float32), lo.astype(jnp.float32))

    def spread(vec, first, count):
        for s in range(first, first + count):
            hi = vec[s].astype(jnp.bfloat16).astype(jnp.float32)
            lay(s, hi, vec[s] - hi)

    def product(rows, ranges):
        columns = [pl.ds(a * SAMP, k * SAMP) for a, k in ranges]
        hi, lo = [jnp.concatenate([e[rows, c] for c in columns], axis=1) for e in (e_hi, e_lo)]
        w = jnp.concatenate([w_all[c, :] for c in columns], axis=0)
        both = jnp.dot(hi, w, preferred_element_type=jnp.float32)
        low = jnp.dot(lo, w[:, 0:128], preferred_element_type=jnp.float32)
        return both[:, 0:128] + both[:, 128:256] + low

    def slots_of(buf, first, count):
        return jnp.concatenate(
            [
                jnp.concatenate([buf[s, SAMP * k : SAMP * k + SAMP, :] for k in range(4)], axis=1)
                for s in range(first, first + count)
            ],
            axis=0,
        )

    def tile(r_first, r_count, ranges):
        left = slots_of(row_st, r_first, r_count)
        right = jnp.concatenate([slots_of(col_st, a, k) for a, k in ranges], axis=0)
        cross = lax.dot_general(left, right, (((1,), (1,)), ((), ())), preferred_element_type=jnp.float32)
        e = jnp.exp2(cross * EXP_SCALE)
        hi = e.astype(jnp.bfloat16)
        lo = (e - hi.astype(jnp.float32)).astype(jnp.bfloat16)
        rows = pl.ds(r_first * SAMP, r_count * SAMP)
        at = 0
        for a, k in ranges:
            columns = pl.ds(a * SAMP, k * SAMP)
            e_hi[rows, columns] = hi[:, at : at + k * SAMP]
            e_lo[rows, columns] = lo[:, at : at + k * SAMP]
            at += k * SAMP

    def grow_own(g):
        first, count = GROUPS[g]
        if first:
            tile(first, count, [(0, first), (16, first)])
        tile(0, first + count, [(first, count)])

    def grow_other(g):
        first, count = GROUPS[g]
        wait(col_st.at[pl.ds(16 + first, count)], s_recv.at[g])
        tile(0, first + count, [(16 + first, count)])

    sides = (-1, 1)
    pair = place(0, 1)
    chains = ((take_col, send_col), (take_row, send_row))
    for take, pass_on in chains:
        take(pair)
        for side in sides:
            pass_on(pair, 2 * side)
        for side in sides:
            pass_on(0, side)
    for take, pass_on in chains:
        for side in sides:
            take(place(2 * side, 0))
            pass_on(place(2 * side, 0), -side)
    share(0)
    grow_own(0)
    grow_other(0)
    for take, pass_on in chains:
        for side in sides:
            take(place(2 * side, 1))
            pass_on(place(2 * side, 1), -side)
        for side in sides:
            pass_on(pair, side)
    for take, pass_on in chains:
        for side in sides:
            take(place(side, 0))
        for side in sides:
            take(place(3 * side, 0))
            pass_on(place(3 * side, 0), -side, half=(side + 1) // 2)
    share(1)
    grow_own(1)
    grow_other(1)
    for take, pass_on in chains:
        for side in sides:
            take(place(3 * side, 1))
            pass_on(place(3 * side, 1), -side, half=(side + 1) // 2)
        for side in sides:
            take(place(side, 1))
    share(2)
    before = GROUPS[2][0]
    grow_own(2)
    for first in (0, 16):
        spread_sent(first, before)
    for first, count in ((0, 256), (256, 256), (512, 128)):
        rows = pl.ds(first, count)
        acc[rows, :] = product(rows, [(0, before), (16, before)])
    grow_other(2)
    for first in (0, 16):
        spread_sent(first + before, SOONER - before)
    for first, count in ((0, 256), (256, 256), (512, 128)):
        rows = pl.ds(first, count)
        acc[rows, :] += product(rows, [(before, SOONER - before), (16 + before, SOONER - before)])
    rows = pl.ds(before * SAMP, (SOONER - before) * SAMP)
    acc[rows, :] = product(rows, [(0, SOONER), (16, SOONER)])
    for a in (0, 1):
        take_col(place(4, a))

    row_far, col_far = far_first(1), far_first(2)

    def to_owner(part, got, s, s_sem, r_sem):
        whole = fold_lanes(acc[SAMP * s : SAMP * s + SAMP, :])
        part[s] = by_group([whole[16 * g : 16 * g + 16] for g in range(4)])
        if s:
            send(part.at[s], got.at[mirror(s)], col_peer(*SLOTS[s]), s_sem, r_sem)

    last = [(SOONER, 2), (16 + SOONER, 2)]
    spread_sent(SOONER, 2)
    spread_sent(16 + SOONER, 2)
    tile(0, SOONER, last)
    for a in (0, 1):
        take_row(place(4, a))
    tile(SOONER, 2, [(0, 32)])
    for first, count in ((14, 2), (10, 4), (6, 4), (4, 2), (0, 4)):
        rows = pl.ds(first * SAMP, count * SAMP)
        if first == SOONER:
            acc[rows, :] = product(rows, [(0, 32)])
        else:
            acc[rows, :] += product(rows, last)
        for s in range(first + count - 1, first - 1, -1):
            to_owner(part1, got1, s, send_sem.at[3], phase_recv.at[0])
    wait(got1.at[pl.ds(1, 15)], phase_recv.at[0])
    total = part1[0]
    for s in range(1, 16):
        total = total + got1[s]
    r0 = target - (scale * total + start)
    weight = scale * r0
    vec1[0] = weight
    vec1r[0] = weight

    for s in row_far:
        at = mirror(s)
        send(vec1.at[0], vec1.at[at], row_peer(*SLOTS[s], 0), send_sem.at[4], phase_recv.at[1 if at < 12 else 2])
    send(vec1.at[0], vec1.at[16], sibling, sib_send.at[2], phase_recv.at[3])
    for s in col_far:
        send(vec1r.at[0], vec1r.at[mirror(s)], col_peer(*SLOTS[s]), send_sem.at[5], phase_recv.at[6])

    def second(first, count, fresh, rows):
        add = product(rows, [(first, count)])
        acc[rows, :] = add if fresh else acc[rows, :] + add

    every = pl.ds(0, 1024)
    wait(vec1.at[pl.ds(1, 11)], phase_recv.at[1])
    send(vec1.at[pl.ds(1, 11)], vec1.at[pl.ds(17, 11)], sibling, sib_send.at[2], phase_recv.at[4])
    spread(vec1, 0, 12)
    second(0, 12, True, every)
    wait(vec1.at[pl.ds(12, 4)], phase_recv.at[2])
    send(vec1.at[pl.ds(12, 4)], vec1.at[pl.ds(28, 4)], sibling, sib_send.at[2], phase_recv.at[5])
    spread(vec1, 12, 4)
    second(12, 4, False, every)
    wait(vec1.at[16], phase_recv.at[3])
    wait(vec1.at[pl.ds(17, 11)], phase_recv.at[4])
    spread(vec1, 16, 12)
    second(16, 12, False, every)
    wait(vec1.at[pl.ds(28, 4)], phase_recv.at[5])
    spread(vec1, 28, 4)
    for chunk in (3, 2, 1, 0):
        second(28, 4, False, pl.ds(256 * chunk, 256))
        for s in range(4 * chunk + 3, 4 * chunk - 1, -1):
            to_owner(part2, got2, s, send_sem.at[6], phase_recv.at[7])

    wait(vec1r.at[pl.ds(1, 15)], phase_recv.at[6])
    bend = vec1r[0] * part2[0]
    for s in range(1, 16):
        bend = bend + vec1r[s] * part2[s]
    bend = jnp.sum(bend, axis=0, keepdims=True)
    squares = jnp.sum(r0 * r0, axis=0, keepdims=True)
    first_row = lax.broadcasted_iota(jnp.int32, (8, 128), 0) == 0
    both = fold_lanes(jnp.where(first_row, jnp.broadcast_to(bend, (8, 128)), jnp.broadcast_to(squares, (8, 128))))
    dots[0] = both
    two = pl.ds(0, 2)
    for s in row_far + [0]:
        for dcore in (1, 0):
            if s or dcore:
                at = 16 * dcore + mirror(s)
                to = row_peer(*SLOTS[s], dcore)
                send(dots.at[0, two], got_dots.at[at, two], to, send_sem.at[7], phase_recv.at[8])
    wait(got_dots.at[pl.ds(1, 31), two], phase_recv.at[8])
    both = both[0:2]
    for s in range(1, 32):
        both = both + got_dots[s, 0:2, :]
    dots[1, 0:2, :] = both
    for s in col_far:
        to = col_peer(*SLOTS[s])
        send(dots.at[1, two], got_dots2.at[mirror(s), two], to, send_sem.at[8], phase_recv.at[9])
    wait(got2.at[pl.ds(1, 15)], phase_recv.at[7])
    total = part2[0]
    for s in range(1, 16):
        total = total + got2[s]
    q = scale * total + r0
    wait(got_dots2.at[pl.ds(1, 15), two], phase_recv.at[9])
    for s in range(1, 16):
        both = both + got_dots2[s, 0:2, :]
    squares = both[1:2]
    alpha = squares / (both[0:1] + squares)
    coef = start + alpha * r0
    res = r0 - alpha * q
    low = lax.broadcasted_iota(jnp.int32, (16, 128), 1) < OUT
    for g in range(4):
        a = pltpu.roll(coef, (128 - OUT * g) % 128, axis=1) if g else coef
        b = pltpu.roll(res, (128 + OUT - OUT * g) % 128, axis=1) if g != 1 else res
        flip[16 * g : 16 * g + 16, :] = jnp.where(low, a, b)
    back = flip[...].T
    both_out[0] = back[0:OUT, 0:SAMP]
    both_out[1] = back[OUT : 2 * OUT, 0:SAMP]

    wait(col_st.at[pl.ds(0, 17)], send_sem.at[0])
    wait(row_st.at[pl.ds(0, 15)], send_sem.at[1])
    wait(col_st.at[pl.ds(0, 14)], sib_send.at[0])
    wait(vec1.at[pl.ds(0, 16)], sib_send.at[2])
    wait(part1.at[pl.ds(0, 15)], send_sem.at[3])
    wait(vec1.at[pl.ds(0, 15)], send_sem.at[4])
    wait(vec1r.at[pl.ds(0, 15)], send_sem.at[5])
    wait(part2.at[pl.ds(0, 15)], send_sem.at[6])
    wait(got_dots.at[pl.ds(0, 31), two], send_sem.at[7])
    wait(got_dots2.at[pl.ds(0, 15), two], send_sem.at[8])


def store(both, coef_out, res_out, sem):
    copies = [pltpu.make_async_copy(both.at[k], out, sem.at[k]) for k, out in enumerate((coef_out, res_out))]
    for copy in copies:
        copy.start()
    for copy in copies:
        copy.wait()


def local(states, targets, start_coef, washout):
    f32, bf16 = jnp.float32, jnp.bfloat16
    vmem = pl.BlockSpec(memory_space=pltpu.VMEM)
    hbm = pl.BlockSpec(memory_space=pltpu.HBM)
    dma = pltpu.SemaphoreType.DMA
    inputs = (states, targets, start_coef, washout.reshape(1, SAMP))
    both = pl.pallas_call(
        kernel,
        out_shape=pltpu.VMEM((2, OUT, SAMP), f32),
        in_specs=[hbm] * 4,
        out_specs=vmem,
        scratch_shapes=[
            pltpu.VMEM((SAMP, DIM), bf16),
            pltpu.VMEM((2, OUT, SAMP), f32),
            pltpu.VMEM((1, SAMP), jnp.int32),
            pltpu.VMEM((32, COL_SLOT, 128), bf16),
            pltpu.VMEM((16, ROW_SLOT, 128), bf16),
            pltpu.VMEM((1024, 2048), bf16),
            pltpu.VMEM((1024, 2048), bf16),
            pltpu.VMEM((2048, 256), bf16),
            pltpu.VMEM((1024, 128), f32),
            pltpu.VMEM((128, 128), f32),
            pltpu.VMEM((16, 16, 128), f32),
            pltpu.VMEM((16, 16, 128), f32),
            pltpu.VMEM((32, 16, 128), f32),
            pltpu.VMEM((16, 16, 128), f32),
            pltpu.VMEM((16, 16, 128), f32),
            pltpu.VMEM((16, 16, 128), f32),
            pltpu.VMEM((2, 8, 128), f32),
            pltpu.VMEM((32, 8, 128), f32),
            pltpu.VMEM((16, 8, 128), f32),
            dma((4,)),
            dma((9,)),
            dma((3,)),
            dma((18,)),
            dma((8,)),
            dma((18,)),
            dma((10,)),
        ],
        compiler_params=pltpu.CompilerParams(
            collective_id=0, has_side_effects=True, vmem_limit_bytes=48 * 1024 * 1024
        ),
    )(*[pltpu.with_memory_space_constraint(x, pltpu.HBM) for x in inputs])
    out = jax.ShapeDtypeStruct((OUT, SAMP), f32)
    return pl.pallas_call(
        store,
        out_shape=(out, out),
        in_specs=[vmem],
        out_specs=(hbm, hbm),
        scratch_shapes=[dma((2,))],
        compiler_params=pltpu.CompilerParams(vmem_limit_bytes=2 * 1024 * 1024),
    )(both)


def solution(mesh):
    return jax.shard_map(
        local,
        mesh=mesh,
        in_specs=(
            P(("row", "col"), None),
            P(None, ("row", "col")),
            P(None, ("row", "col")),
            P(("row", "col")),
        ),
        out_specs=(P(None, ("row", "col")), P(None, ("row", "col"))),
        check_vma=False,
    )
```

```python
import math

import jax
import jax.numpy as jnp
from jax import lax
from jax.experimental import pallas as pl
from jax.experimental.pallas import tpu as pltpu
from jax.sharding import PartitionSpec as P

MESH = pl.DeviceIdType.MESH
RING = 8
SAMP = 64
DIM = 512
OUT = 32
SLOTS = [
    (0, 0), (0, 1), (-2, 0), (2, 0),
    (-1, 0), (1, 0), (-2, 1), (2, 1), (-3, 0), (3, 0),
    (-1, 1), (1, 1), (-3, 1), (3, 1),
    (4, 0), (4, 1),
]
INDEX = {slot: at for at, slot in enumerate(SLOTS)}
GROUPS = [(0, 4), (4, 6), (10, 4)]
SOONER = 14
ROW_SLOT = 4 * SAMP
COL_SLOT = ROW_SLOT + 32
EXP_SCALE = math.log2(math.e) * 2.0 / DIM


def place(d, a):
    return INDEX[(d + RING // 2 - 1) % RING - RING // 2 + 1, a % 2]


def mirror(s):
    return place(-SLOTS[s][0], SLOTS[s][1])


CHIPS = sorted(
    [(dx, dy, dz) for dx in range(4) for dy in range(RING) for dz in range(RING) if dx or dy or dz],
    key=lambda d: -min(d[0], 4 - d[0]) - min(d[1], RING - d[1]) - min(d[2], RING - d[2]),
)


def far_first(pair_hops):
    return sorted(range(1, 16), key=lambda s: -abs(SLOTS[s][0]) - pair_hops * SLOTS[s][1])


def lane_group():
    return lax.broadcasted_iota(jnp.int32, (16, 128), 1) // OUT


def by_group(pieces):
    group = lane_group()
    out = pieces[3]
    for g in (2, 1, 0):
        out = jnp.where(group == g, pieces[g], out)
    return out


def pack(block, at):
    return by_group(
        [
            pltpu.roll(block[16 * g : 16 * g + 16], (OUT * (g - at)) % 128, axis=1)
            if g != at
            else block[16 * g : 16 * g + 16]
            for g in range(4)
        ]
    )


def fold_lanes(x):
    x = x + pltpu.roll(x, 64, axis=1)
    return x + pltpu.roll(x, 32, axis=1)


def kernel(
    states_in, targets_in, coef_in, washout_in,
    both_out,
    states, vectors, washout, col_st, row_st, e_hi, e_lo, w_all, acc, flip,
    part1, got1, vec1, vec1r, part2, got2, dots, got_dots, got_dots2,
    in_sem, send_sem, sib_send, c_recv, s_recv, r_recv, phase_recv,
):
    row, col = lax.axis_index("row"), lax.axis_index("col")
    core, xl, y = row % 2, (row // 2) % 2, row // 4
    xh, z = col % 2, col // 2

    def row_peer(dy, dxl, dcore):
        return (((y + dy + RING) % RING * 2 + (xl + dxl) % 2) * 2 + (core + dcore) % 2, col)

    def col_peer(dz, dxh):
        return (row, (z + dz + RING) % RING * 2 + (xh + dxh) % 2)

    sibling = row_peer(0, 0, 1)
    near = [row_peer(1, 0, 0), row_peer(-1, 0, 0), row_peer(0, 1, 0), sibling]
    near += [col_peer(1, 0), col_peer(-1, 0), col_peer(0, 1)]
    near += [row_peer(2, 0, 0), row_peer(-2, 0, 0), col_peer(2, 0), col_peer(-2, 0)]

    barrier = pltpu.get_barrier_semaphore()
    for who in near:
        pl.semaphore_signal(barrier, inc=1, device_id=who, device_id_type=MESH)

    fetches = [
        pltpu.make_async_copy(states_in, states, in_sem.at[0]),
        pltpu.make_async_copy(targets_in, vectors.at[0], in_sem.at[1]),
        pltpu.make_async_copy(coef_in, vectors.at[1], in_sem.at[2]),
        pltpu.make_async_copy(washout_in, washout, in_sem.at[3]),
    ]
    for fetch in fetches:
        fetch.start()
    fetches[0].wait()

    def send(src, dst, to, s_sem, r_sem):
        pltpu.make_async_remote_copy(
            src_ref=src, dst_ref=dst, send_sem=s_sem, recv_sem=r_sem, device_id=to, device_id_type=MESH
        ).start()

    def wait(ref, sem):
        pltpu.make_async_copy(ref, ref, sem).wait()

    def send_col(s, d, a=0, half=None):
        to = place(SLOTS[s][0] - d, SLOTS[s][1] + a)
        rows = pl.ds(0, COL_SLOT) if half is None else pl.ds(half * (COL_SLOT // 2), COL_SLOT // 2)
        sem = 16 + SLOTS[to][1] if half else to
        src = col_st.at[s, rows]
        send(src, col_st.at[to, rows], row_peer(d, a, 0), send_sem.at[0], c_recv.at[sem])
        if half is not None:
            both = s_recv.at[4 + 2 * half + SLOTS[to][1]]
            send(src, col_st.at[16 + to, rows], row_peer(d, a, 1), send_sem.at[0], both)

    def send_row(s, d, a=0, half=None):
        to = place(SLOTS[s][0] - d, SLOTS[s][1] + a)
        rows = pl.ds(0, ROW_SLOT) if half is None else pl.ds(half * (ROW_SLOT // 2), ROW_SLOT // 2)
        sem = 16 + SLOTS[to][1] if half else to
        send(row_st.at[s, rows], row_st.at[to, rows], col_peer(d, a), send_sem.at[1], r_recv.at[sem])

    def take_col(s):
        if SLOTS[s][0] == 4:
            for half in (0, 1):
                rows = pl.ds(half * (COL_SLOT // 2), COL_SLOT // 2)
                wait(col_st.at[s, rows], c_recv.at[16 + SLOTS[s][1] if half else s])
                wait(col_st.at[16 + s, rows], s_recv.at[4 + 2 * half + SLOTS[s][1]])
        else:
            wait(col_st.at[s], c_recv.at[s])

    def take_row(s):
        if SLOTS[s][0] == 4:
            for half in (0, 1):
                rows = pl.ds(half * (ROW_SLOT // 2), ROW_SLOT // 2)
                wait(row_st.at[s, rows], r_recv.at[16 + SLOTS[s][1] if half else s])
        else:
            wait(row_st.at[s], r_recv.at[s])

    def share(g):
        first, count = GROUPS[g]
        own, other = pl.ds(first, count), pl.ds(16 + first, count)
        send(col_st.at[own], col_st.at[other], sibling, sib_send.at[0], s_recv.at[g])

    for k in range(4):
        piece = states[:, 128 * k : 128 * k + 128]
        col_st[0, SAMP * k : SAMP * k + SAMP, :] = piece
        row_st[0, SAMP * k : SAMP * k + SAMP, :] = piece
    own_f = states[...].astype(jnp.float32)
    norm = jnp.sum(own_f * own_f, axis=1, keepdims=True)
    damp_col = jnp.broadcast_to(jnp.exp(norm * (-1.0 / DIM)), (SAMP, 128))
    damp = by_group([damp_col[16 * g : 16 * g + 16] for g in range(4)])
    for fetch in fetches[1:]:
        fetch.wait()
    flip[0:OUT, 0:SAMP] = vectors[0]
    flip[OUT : 2 * OUT, 0:SAMP] = vectors[1]
    flip[2 * OUT : 3 * OUT, 0:SAMP] = jnp.broadcast_to(washout[...].astype(jnp.float32), (OUT, SAMP))
    turned = flip[...].T[0:SAMP]
    mask = pack(turned, 2)
    target = pack(turned, 0) * mask
    start = pack(turned, 1)
    scale = mask * damp
    weight = scale * start
    high = weight.astype(jnp.bfloat16)
    col_st[0, ROW_SLOT : ROW_SLOT + 16, :] = high
    col_st[0, ROW_SLOT + 16 : COL_SLOT, :] = (weight - high.astype(jnp.float32)).astype(jnp.bfloat16)
    pl.semaphore_wait(barrier, len(near))

    for way in (send_col, send_row):
        way(0, 0, 1)
        way(0, 2)
        way(0, -2)

    group = lane_group()

    def lay(s, hi, lo):
        for g in range(4):
            keep = group == g
            at = SAMP * s + 16 * g
            w_all[at : at + 16, 0:128] = jnp.where(keep, hi, 0.0).astype(jnp.bfloat16)
            w_all[at : at + 16, 128:256] = jnp.where(keep, lo, 0.0).astype(jnp.bfloat16)

    def spread_sent(first, count):
        for s in range(first, first + count):
            hi = col_st[s, ROW_SLOT : ROW_SLOT + 16, :]
            lo = col_st[s, ROW_SLOT + 16 : COL_SLOT, :]
            lay(s, hi.astype(jnp.float32), lo.astype(jnp.float32))

    def spread(vec, first, count):
        for s in range(first, first + count):
            hi = vec[s].astype(jnp.bfloat16).astype(jnp.float32)
            lay(s, hi, vec[s] - hi)

    def product(rows, ranges):
        columns = [pl.ds(a * SAMP, k * SAMP) for a, k in ranges]
        hi, lo = [jnp.concatenate([e[rows, c] for c in columns], axis=1) for e in (e_hi, e_lo)]
        w = jnp.concatenate([w_all[c, :] for c in columns], axis=0)
        both = jnp.dot(hi, w, preferred_element_type=jnp.float32)
        low = jnp.dot(lo, w[:, 0:128], preferred_element_type=jnp.float32)
        return both[:, 0:128] + both[:, 128:256] + low

    def slots_of(buf, first, count):
        return jnp.concatenate(
            [
                jnp.concatenate([buf[s, SAMP * k : SAMP * k + SAMP, :] for k in range(4)], axis=1)
                for s in range(first, first + count)
            ],
            axis=0,
        )

    def tile(r_first, r_count, ranges):
        left = slots_of(row_st, r_first, r_count)
        right = jnp.concatenate([slots_of(col_st, a, k) for a, k in ranges], axis=0)
        cross = lax.dot_general(left, right, (((1,), (1,)), ((), ())), preferred_element_type=jnp.float32)
        e = jnp.exp2(cross * EXP_SCALE)
        hi = e.astype(jnp.bfloat16)
        lo = (e - hi.astype(jnp.float32)).astype(jnp.bfloat16)
        rows = pl.ds(r_first * SAMP, r_count * SAMP)
        at = 0
        for a, k in ranges:
            columns = pl.ds(a * SAMP, k * SAMP)
            e_hi[rows, columns] = hi[:, at : at + k * SAMP]
            e_lo[rows, columns] = lo[:, at : at + k * SAMP]
            at += k * SAMP

    def grow_own(g):
        first, count = GROUPS[g]
        if first:
            tile(first, count, [(0, first), (16, first)])
        tile(0, first + count, [(first, count)])

    def grow_other(g):
        first, count = GROUPS[g]
        wait(col_st.at[pl.ds(16 + first, count)], s_recv.at[g])
        tile(0, first + count, [(16 + first, count)])

    sides = (-1, 1)
    pair = place(0, 1)
    chains = ((take_col, send_col), (take_row, send_row))
    for take, pass_on in chains:
        take(pair)
        for side in sides:
            pass_on(pair, 2 * side)
        for side in sides:
            pass_on(0, side)
    for take, pass_on in chains:
        for side in sides:
            take(place(2 * side, 0))
            pass_on(place(2 * side, 0), -side)
    share(0)
    grow_own(0)
    grow_other(0)
    for take, pass_on in chains:
        for side in sides:
            take(place(2 * side, 1))
            pass_on(place(2 * side, 1), -side)
        for side in sides:
            pass_on(pair, side)
    for take, pass_on in chains:
        for side in sides:
            take(place(side, 0))
        for side in sides:
            take(place(3 * side, 0))
            pass_on(place(3 * side, 0), -side, half=(side + 1) // 2)
    share(1)
    grow_own(1)
    grow_other(1)
    for take, pass_on in chains:
        for side in sides:
            take(place(3 * side, 1))
            pass_on(place(3 * side, 1), -side, half=(side + 1) // 2)
        for side in sides:
            take(place(side, 1))
    share(2)
    before = GROUPS[2][0]
    grow_own(2)
    for first in (0, 16):
        spread_sent(first, before)
    for first, count in ((0, 256), (256, 256), (512, 128)):
        rows = pl.ds(first, count)
        acc[rows, :] = product(rows, [(0, before), (16, before)])
    grow_other(2)
    for first in (0, 16):
        spread_sent(first + before, SOONER - before)
    for first, count in ((0, 256), (256, 256), (512, 128)):
        rows = pl.ds(first, count)
        acc[rows, :] += product(rows, [(before, SOONER - before), (16 + before, SOONER - before)])
    rows = pl.ds(before * SAMP, (SOONER - before) * SAMP)
    acc[rows, :] = product(rows, [(0, SOONER), (16, SOONER)])
    for a in (0, 1):
        take_col(place(4, a))

    row_far, col_far = far_first(1), far_first(2)

    def to_owner(part, got, s, s_sem, r_sem):
        whole = fold_lanes(acc[SAMP * s : SAMP * s + SAMP, :])
        part[s] = by_group([whole[16 * g : 16 * g + 16] for g in range(4)])
        if s:
            send(part.at[s], got.at[mirror(s)], col_peer(*SLOTS[s]), s_sem, r_sem)

    last = [(SOONER, 2), (16 + SOONER, 2)]
    spread_sent(SOONER, 2)
    spread_sent(16 + SOONER, 2)
    tile(0, SOONER, last)
    for a in (0, 1):
        take_row(place(4, a))
    tile(SOONER, 2, [(0, 32)])
    for first, count in ((14, 2), (10, 4), (6, 4), (4, 2), (0, 4)):
        rows = pl.ds(first * SAMP, count * SAMP)
        if first == SOONER:
            acc[rows, :] = product(rows, [(0, 32)])
        else:
            acc[rows, :] += product(rows, last)
        for s in range(first + count - 1, first - 1, -1):
            to_owner(part1, got1, s, send_sem.at[3], phase_recv.at[0])
    wait(got1.at[pl.ds(1, 15)], phase_recv.at[0])
    total = part1[0]
    for s in range(1, 16):
        total = total + got1[s]
    r0 = target - (scale * total + start)
    weight = scale * r0
    vec1[0] = weight
    vec1r[0] = weight

    for s in row_far:
        at = mirror(s)
        send(vec1.at[0], vec1.at[at], row_peer(*SLOTS[s], 0), send_sem.at[4], phase_recv.at[1 if at < 12 else 2])
    send(vec1.at[0], vec1.at[16], sibling, sib_send.at[2], phase_recv.at[3])
    for s in col_far:
        send(vec1r.at[0], vec1r.at[mirror(s)], col_peer(*SLOTS[s]), send_sem.at[5], phase_recv.at[6])

    def second(first, count, fresh, rows):
        add = product(rows, [(first, count)])
        acc[rows, :] = add if fresh else acc[rows, :] + add

    every = pl.ds(0, 1024)
    wait(vec1.at[pl.ds(1, 11)], phase_recv.at[1])
    send(vec1.at[pl.ds(1, 11)], vec1.at[pl.ds(17, 11)], sibling, sib_send.at[2], phase_recv.at[4])
    spread(vec1, 0, 12)
    second(0, 12, True, every)
    wait(vec1.at[pl.ds(12, 4)], phase_recv.at[2])
    send(vec1.at[pl.ds(12, 4)], vec1.at[pl.ds(28, 4)], sibling, sib_send.at[2], phase_recv.at[5])
    spread(vec1, 12, 4)
    second(12, 4, False, every)
    wait(vec1.at[16], phase_recv.at[3])
    wait(vec1.at[pl.ds(17, 11)], phase_recv.at[4])
    spread(vec1, 16, 12)
    second(16, 12, False, every)
    wait(vec1.at[pl.ds(28, 4)], phase_recv.at[5])
    spread(vec1, 28, 4)
    for chunk in (3, 2, 1, 0):
        second(28, 4, False, pl.ds(256 * chunk, 256))
        for s in range(4 * chunk + 3, 4 * chunk - 1, -1):
            to_owner(part2, got2, s, send_sem.at[6], phase_recv.at[7])

    wait(vec1r.at[pl.ds(1, 15)], phase_recv.at[6])
    bend = vec1r[0] * part2[0]
    for s in range(1, 16):
        bend = bend + vec1r[s] * part2[s]
    bend = jnp.sum(bend, axis=0, keepdims=True)
    squares = jnp.sum(r0 * r0, axis=0, keepdims=True)
    leading = lax.broadcasted_iota(jnp.int32, (1, 128), 1) < OUT
    line = jnp.where(leading, fold_lanes(bend), fold_lanes(squares))
    dots[0:1, :] = line
    got_dots[0:1, :] = line
    x = xh * 2 + xl
    at_x = [(x + d) % 4 for d in range(4)]
    rows_x = [(v % 2) * 2 + core for v in at_x]
    cols_x = [v // 2 for v in at_x]
    rows_y = [(y + d) % RING * 4 for d in range(RING)]
    cols_z = [(z + d) % RING * 2 for d in range(RING)]
    for dx, dy, dz in CHIPS:
        back = (-dx % 4 * RING + -dy % RING) * RING + -dz % RING
        to = (rows_y[dy] + rows_x[dx], cols_z[dz] + cols_x[dx])
        send(dots.at[pl.ds(0, 1)], got_dots.at[pl.ds(back, 1)], to, send_sem.at[7], phase_recv.at[8])
    wait(got2.at[pl.ds(1, 15)], phase_recv.at[7])
    total = part2[0]
    for s in range(1, 16):
        total = total + got2[s]
    q = scale * total + r0
    wait(got_dots.at[pl.ds(1, 255)], phase_recv.at[8])
    line = jnp.sum(jnp.sum(got_dots[...].reshape(32, 8, 128), axis=0), axis=0, keepdims=True)
    dots[1:2, :] = line
    send(dots.at[pl.ds(1, 1)], got_dots2.at[pl.ds(0, 1)], sibling, send_sem.at[8], phase_recv.at[9])
    wait(got_dots2.at[pl.ds(0, 1)], phase_recv.at[9])
    line = line + got_dots2[0:1, :]
    bend = fold_lanes(jnp.where(leading, line, 0.0))
    squares = jnp.where(leading, pltpu.roll(line, 128 - OUT, axis=1), line)
    alpha = squares / (bend + squares)
    coef = start + alpha * r0
    res = r0 - alpha * q
    low = lax.broadcasted_iota(jnp.int32, (16, 128), 1) < OUT
    for g in range(4):
        a = pltpu.roll(coef, (128 - OUT * g) % 128, axis=1) if g else coef
        b = pltpu.roll(res, (128 + OUT - OUT * g) % 128, axis=1) if g != 1 else res
        flip[16 * g : 16 * g + 16, :] = jnp.where(low, a, b)
    back = flip[...].T
    both_out[0] = back[0:OUT, 0:SAMP]
    both_out[1] = back[OUT : 2 * OUT, 0:SAMP]

    wait(col_st.at[pl.ds(0, 17)], send_sem.at[0])
    wait(row_st.at[pl.ds(0, 15)], send_sem.at[1])
    wait(col_st.at[pl.ds(0, 14)], sib_send.at[0])
    wait(vec1.at[pl.ds(0, 16)], sib_send.at[2])
    wait(part1.at[pl.ds(0, 15)], send_sem.at[3])
    wait(vec1.at[pl.ds(0, 15)], send_sem.at[4])
    wait(vec1r.at[pl.ds(0, 15)], send_sem.at[5])
    wait(part2.at[pl.ds(0, 15)], send_sem.at[6])
    wait(got_dots.at[pl.ds(0, 255)], send_sem.at[7])
    wait(got_dots2.at[pl.ds(0, 1)], send_sem.at[8])


def store(both, coef_out, res_out, sem):
    copies = [pltpu.make_async_copy(both.at[k], out, sem.at[k]) for k, out in enumerate((coef_out, res_out))]
    for copy in copies:
        copy.start()
    for copy in copies:
        copy.wait()


def local(states, targets, start_coef, washout):
    f32, bf16 = jnp.float32, jnp.bfloat16
    vmem = pl.BlockSpec(memory_space=pltpu.VMEM)
    hbm = pl.BlockSpec(memory_space=pltpu.HBM)
    dma = pltpu.SemaphoreType.DMA
    inputs = (states, targets, start_coef, washout.reshape(1, SAMP))
    both = pl.pallas_call(
        kernel,
        out_shape=pltpu.VMEM((2, OUT, SAMP), f32),
        in_specs=[hbm] * 4,
        out_specs=vmem,
        scratch_shapes=[
            pltpu.VMEM((SAMP, DIM), bf16),
            pltpu.VMEM((2, OUT, SAMP), f32),
            pltpu.VMEM((1, SAMP), jnp.int32),
            pltpu.VMEM((32, COL_SLOT, 128), bf16),
            pltpu.VMEM((16, ROW_SLOT, 128), bf16),
            pltpu.VMEM((1024, 2048), bf16),
            pltpu.VMEM((1024, 2048), bf16),
            pltpu.VMEM((2048, 256), bf16),
            pltpu.VMEM((1024, 128), f32),
            pltpu.VMEM((128, 128), f32),
            pltpu.VMEM((16, 16, 128), f32),
            pltpu.VMEM((16, 16, 128), f32),
            pltpu.VMEM((32, 16, 128), f32),
            pltpu.VMEM((16, 16, 128), f32),
            pltpu.VMEM((16, 16, 128), f32),
            pltpu.VMEM((16, 16, 128), f32),
            pltpu.VMEM((8, 128), f32),
            pltpu.VMEM((256, 128), f32),
            pltpu.VMEM((8, 128), f32),
            dma((4,)),
            dma((9,)),
            dma((3,)),
            dma((18,)),
            dma((8,)),
            dma((18,)),
            dma((10,)),
        ],
        compiler_params=pltpu.CompilerParams(
            collective_id=0, has_side_effects=True, vmem_limit_bytes=48 * 1024 * 1024
        ),
    )(*[pltpu.with_memory_space_constraint(x, pltpu.HBM) for x in inputs])
    out = jax.ShapeDtypeStruct((OUT, SAMP), f32)
    return pl.pallas_call(
        store,
        out_shape=(out, out),
        in_specs=[vmem],
        out_specs=(hbm, hbm),
        scratch_shapes=[dma((2,))],
        compiler_params=pltpu.CompilerParams(vmem_limit_bytes=2 * 1024 * 1024),
    )(both)


def solution(mesh):
    return jax.shard_map(
        local,
        mesh=mesh,
        in_specs=(
            P(("row", "col"), None),
            P(None, ("row", "col")),
            P(None, ("row", "col")),
            P(("row", "col")),
        ),
        out_specs=(P(None, ("row", "col")), P(None, ("row", "col"))),
        check_vma=False,
    )
```

```python
import math

import jax
import jax.numpy as jnp
from jax import lax
from jax.experimental import pallas as pl
from jax.experimental.pallas import tpu as pltpu
from jax.sharding import PartitionSpec as P

MESH = pl.DeviceIdType.MESH
RING = 8
SAMP = 64
DIM = 512
OUT = 32
SLOTS = [
    (0, 0), (0, 1), (-2, 0), (2, 0),
    (-1, 0), (1, 0), (-2, 1), (2, 1), (-3, 0), (3, 0),
    (-1, 1), (1, 1), (-3, 1), (3, 1),
    (4, 0), (4, 1),
]
INDEX = {slot: at for at, slot in enumerate(SLOTS)}
GROUPS = [(0, 4), (4, 6), (10, 4)]
SOONER = 14
ROW_SLOT = 4 * SAMP
COL_SLOT = ROW_SLOT + 32
EXP_SCALE = math.log2(math.e) * 2.0 / DIM


def place(d, a):
    return INDEX[(d + RING // 2 - 1) % RING - RING // 2 + 1, a % 2]


def mirror(s):
    return place(-SLOTS[s][0], SLOTS[s][1])


CHIPS = sorted(
    [(dx, dy, dz) for dx in range(4) for dy in range(RING) for dz in range(RING) if dx or dy or dz],
    key=lambda d: -min(d[0], 4 - d[0]) - min(d[1], RING - d[1]) - min(d[2], RING - d[2]),
)


def far_first(pair_hops):
    return sorted(range(1, 16), key=lambda s: -abs(SLOTS[s][0]) - pair_hops * SLOTS[s][1])


def lane_group():
    return lax.broadcasted_iota(jnp.int32, (16, 128), 1) // OUT


def by_group(pieces):
    group = lane_group()
    out = pieces[3]
    for g in (2, 1, 0):
        out = jnp.where(group == g, pieces[g], out)
    return out


def pack(block, at):
    return by_group(
        [
            pltpu.roll(block[16 * g : 16 * g + 16], (OUT * (g - at)) % 128, axis=1)
            if g != at
            else block[16 * g : 16 * g + 16]
            for g in range(4)
        ]
    )


def fold_lanes(x):
    x = x + pltpu.roll(x, 64, axis=1)
    return x + pltpu.roll(x, 32, axis=1)


def kernel(
    states_in, targets_in, coef_in, washout_in,
    both_out,
    states, vectors, washout, col_st, row_st, e_hi, e_lo, w_all, acc, flip,
    part1, got1, vec1, vec1r, part2, got2, dots, got_dots, got_dots2,
    in_sem, send_sem, sib_send, c_recv, s_recv, r_recv, phase_recv,
):
    row, col = lax.axis_index("row"), lax.axis_index("col")
    core, xl, y = row % 2, (row // 2) % 2, row // 4
    xh, z = col % 2, col // 2

    def row_peer(dy, dxl, dcore):
        return (((y + dy + RING) % RING * 2 + (xl + dxl) % 2) * 2 + (core + dcore) % 2, col)

    def col_peer(dz, dxh):
        return (row, (z + dz + RING) % RING * 2 + (xh + dxh) % 2)

    sibling = row_peer(0, 0, 1)
    near = [row_peer(1, 0, 0), row_peer(-1, 0, 0), row_peer(0, 1, 0), sibling]
    near += [col_peer(1, 0), col_peer(-1, 0), col_peer(0, 1)]
    near += [row_peer(2, 0, 0), row_peer(-2, 0, 0), col_peer(2, 0), col_peer(-2, 0)]

    barrier = pltpu.get_barrier_semaphore()
    for who in near:
        pl.semaphore_signal(barrier, inc=1, device_id=who, device_id_type=MESH)

    fetches = [
        pltpu.make_async_copy(states_in, states, in_sem.at[0]),
        pltpu.make_async_copy(targets_in, vectors.at[0], in_sem.at[1]),
        pltpu.make_async_copy(coef_in, vectors.at[1], in_sem.at[2]),
        pltpu.make_async_copy(washout_in, washout, in_sem.at[3]),
    ]
    for fetch in fetches:
        fetch.start()

    def send(src, dst, to, s_sem, r_sem):
        pltpu.make_async_remote_copy(
            src_ref=src, dst_ref=dst, send_sem=s_sem, recv_sem=r_sem, device_id=to, device_id_type=MESH
        ).start()

    def wait(ref, sem):
        pltpu.make_async_copy(ref, ref, sem).wait()

    def send_col(s, d, a=0, half=None):
        to = place(SLOTS[s][0] - d, SLOTS[s][1] + a)
        rows = pl.ds(0, COL_SLOT) if half is None else pl.ds(half * (COL_SLOT // 2), COL_SLOT // 2)
        sem = 16 + SLOTS[to][1] if half else to
        src = col_st.at[s, rows]
        send(src, col_st.at[to, rows], row_peer(d, a, 0), send_sem.at[0], c_recv.at[sem])
        if half is not None:
            both = s_recv.at[4 + 2 * half + SLOTS[to][1]]
            send(src, col_st.at[16 + to, rows], row_peer(d, a, 1), send_sem.at[0], both)

    def send_row(s, d, a=0, half=None):
        to = place(SLOTS[s][0] - d, SLOTS[s][1] + a)
        rows = pl.ds(0, ROW_SLOT) if half is None else pl.ds(half * (ROW_SLOT // 2), ROW_SLOT // 2)
        sem = 16 + SLOTS[to][1] if half else to
        send(row_st.at[s, rows], row_st.at[to, rows], col_peer(d, a), send_sem.at[1], r_recv.at[sem])

    def take_col(s):
        if SLOTS[s][0] == 4:
            for half in (0, 1):
                rows = pl.ds(half * (COL_SLOT // 2), COL_SLOT // 2)
                wait(col_st.at[s, rows], c_recv.at[16 + SLOTS[s][1] if half else s])
                wait(col_st.at[16 + s, rows], s_recv.at[4 + 2 * half + SLOTS[s][1]])
        else:
            wait(col_st.at[s], c_recv.at[s])

    def take_row(s):
        if SLOTS[s][0] == 4:
            for half in (0, 1):
                rows = pl.ds(half * (ROW_SLOT // 2), ROW_SLOT // 2)
                wait(row_st.at[s, rows], r_recv.at[16 + SLOTS[s][1] if half else s])
        else:
            wait(row_st.at[s], r_recv.at[s])

    def share(g):
        first, count = GROUPS[g]
        own, other = pl.ds(first, count), pl.ds(16 + first, count)
        send(col_st.at[own], col_st.at[other], sibling, sib_send.at[0], s_recv.at[g])

    pl.semaphore_wait(barrier, len(near))
    first_ways = [(0, 1), (2, 0), (-2, 0)]
    for d, a in first_ways:
        to = place(-d, a)
        for k in range(4):
            piece = states_in.at[:, pl.ds(128 * k, 128)]
            rows = pl.ds(SAMP * k, SAMP)
            send(piece, col_st.at[to, rows], row_peer(d, a, 0), send_sem.at[0], c_recv.at[to])
            send(piece, row_st.at[to, rows], col_peer(d, a), send_sem.at[1], r_recv.at[to])
    fetches[0].wait()

    for k in range(4):
        piece = states[:, 128 * k : 128 * k + 128]
        col_st[0, SAMP * k : SAMP * k + SAMP, :] = piece
        row_st[0, SAMP * k : SAMP * k + SAMP, :] = piece
    own_f = states[...].astype(jnp.float32)
    norm = jnp.sum(own_f * own_f, axis=1, keepdims=True)
    damp_col = jnp.broadcast_to(jnp.exp(norm * (-1.0 / DIM)), (SAMP, 128))
    damp = by_group([damp_col[16 * g : 16 * g + 16] for g in range(4)])
    for fetch in fetches[1:]:
        fetch.wait()
    flip[0:OUT, 0:SAMP] = vectors[0]
    flip[OUT : 2 * OUT, 0:SAMP] = vectors[1]
    flip[2 * OUT : 3 * OUT, 0:SAMP] = jnp.broadcast_to(washout[...].astype(jnp.float32), (OUT, SAMP))
    turned = flip[...].T[0:SAMP]
    mask = pack(turned, 2)
    target = pack(turned, 0) * mask
    start = pack(turned, 1)
    scale = mask * damp
    weight = scale * start
    high = weight.astype(jnp.bfloat16)
    col_st[0, ROW_SLOT : ROW_SLOT + 16, :] = high
    col_st[0, ROW_SLOT + 16 : COL_SLOT, :] = (weight - high.astype(jnp.float32)).astype(jnp.bfloat16)
    for d, a in first_ways:
        rows = pl.ds(ROW_SLOT, 32)
        to = place(-d, a)
        send(col_st.at[0, rows], col_st.at[to, rows], row_peer(d, a, 0), send_sem.at[0], c_recv.at[to])

    group = lane_group()

    def lay(s, hi, lo):
        for g in range(4):
            keep = group == g
            at = SAMP * s + 16 * g
            w_all[at : at + 16, 0:128] = jnp.where(keep, hi, 0.0).astype(jnp.bfloat16)
            w_all[at : at + 16, 128:256] = jnp.where(keep, lo, 0.0).astype(jnp.bfloat16)

    def spread_sent(first, count):
        for s in range(first, first + count):
            hi = col_st[s, ROW_SLOT : ROW_SLOT + 16, :]
            lo = col_st[s, ROW_SLOT + 16 : COL_SLOT, :]
            lay(s, hi.astype(jnp.float32), lo.astype(jnp.float32))

    def spread(vec, first, count):
        for s in range(first, first + count):
            hi = vec[s].astype(jnp.bfloat16).astype(jnp.float32)
            lay(s, hi, vec[s] - hi)

    def product(rows, ranges):
        columns = [pl.ds(a * SAMP, k * SAMP) for a, k in ranges]
        hi, lo = [jnp.concatenate([e[rows, c] for c in columns], axis=1) for e in (e_hi, e_lo)]
        w = jnp.concatenate([w_all[c, :] for c in columns], axis=0)
        both = jnp.dot(hi, w, preferred_element_type=jnp.float32)
        low = jnp.dot(lo, w[:, 0:128], preferred_element_type=jnp.float32)
        return both[:, 0:128] + both[:, 128:256] + low

    def slots_of(buf, first, count):
        return jnp.concatenate(
            [
                jnp.concatenate([buf[s, SAMP * k : SAMP * k + SAMP, :] for k in range(4)], axis=1)
                for s in range(first, first + count)
            ],
            axis=0,
        )

    def tile(r_first, r_count, ranges):
        left = slots_of(row_st, r_first, r_count)
        right = jnp.concatenate([slots_of(col_st, a, k) for a, k in ranges], axis=0)
        cross = lax.dot_general(left, right, (((1,), (1,)), ((), ())), preferred_element_type=jnp.float32)
        e = jnp.exp2(cross * EXP_SCALE)
        hi = e.astype(jnp.bfloat16)
        lo = (e - hi.astype(jnp.float32)).astype(jnp.bfloat16)
        rows = pl.ds(r_first * SAMP, r_count * SAMP)
        at = 0
        for a, k in ranges:
            columns = pl.ds(a * SAMP, k * SAMP)
            e_hi[rows, columns] = hi[:, at : at + k * SAMP]
            e_lo[rows, columns] = lo[:, at : at + k * SAMP]
            at += k * SAMP

    def grow_own(g):
        first, count = GROUPS[g]
        if first:
            tile(first, count, [(0, first), (16, first)])
        tile(0, first + count, [(first, count)])

    def grow_other(g):
        first, count = GROUPS[g]
        wait(col_st.at[pl.ds(16 + first, count)], s_recv.at[g])
        tile(0, first + count, [(16 + first, count)])

    sides = (-1, 1)
    pair = place(0, 1)
    chains = ((take_col, send_col), (take_row, send_row))
    for take, pass_on in chains:
        take(pair)
        for side in sides:
            pass_on(pair, 2 * side)
        for side in sides:
            pass_on(0, side)
    for take, pass_on in chains:
        for side in sides:
            take(place(2 * side, 0))
            pass_on(place(2 * side, 0), -side)
    share(0)
    grow_own(0)
    grow_other(0)
    for take, pass_on in chains:
        for side in sides:
            take(place(2 * side, 1))
            pass_on(place(2 * side, 1), -side)
        for side in sides:
            pass_on(pair, side)
    for take, pass_on in chains:
        for side in sides:
            take(place(side, 0))
        for side in sides:
            take(place(3 * side, 0))
            pass_on(place(3 * side, 0), -side, half=(side + 1) // 2)
    share(1)
    grow_own(1)
    grow_other(1)
    for take, pass_on in chains:
        for side in sides:
            take(place(3 * side, 1))
            pass_on(place(3 * side, 1), -side, half=(side + 1) // 2)
        for side in sides:
            take(place(side, 1))
    share(2)
    before = GROUPS[2][0]
    grow_own(2)
    for first in (0, 16):
        spread_sent(first, before)
    for first, count in ((0, 256), (256, 256), (512, 128)):
        rows = pl.ds(first, count)
        acc[rows, :] = product(rows, [(0, before), (16, before)])
    grow_other(2)
    for first in (0, 16):
        spread_sent(first + before, SOONER - before)
    for first, count in ((0, 256), (256, 256), (512, 128)):
        rows = pl.ds(first, count)
        acc[rows, :] += product(rows, [(before, SOONER - before), (16 + before, SOONER - before)])
    rows = pl.ds(before * SAMP, (SOONER - before) * SAMP)
    acc[rows, :] = product(rows, [(0, SOONER), (16, SOONER)])
    for a in (0, 1):
        take_col(place(4, a))

    row_far, col_far = far_first(1), far_first(2)

    def to_owner(part, got, s, s_sem, r_sem):
        whole = fold_lanes(acc[SAMP * s : SAMP * s + SAMP, :])
        part[s] = by_group([whole[16 * g : 16 * g + 16] for g in range(4)])
        if s:
            send(part.at[s], got.at[mirror(s)], col_peer(*SLOTS[s]), s_sem, r_sem)

    last = [(SOONER, 2), (16 + SOONER, 2)]
    spread_sent(SOONER, 2)
    spread_sent(16 + SOONER, 2)
    for a in (0, 1):
        take_row(place(4, a))
    tile(SOONER, 2, [(0, 32)])
    for first, count in ((14, 2), (10, 4), (6, 4), (4, 2), (0, 4)):
        rows = pl.ds(first * SAMP, count * SAMP)
        if first == SOONER:
            acc[rows, :] = product(rows, [(0, 32)])
        else:
            tile(first, count, last)
            acc[rows, :] += product(rows, last)
        for s in range(first + count - 1, first - 1, -1):
            to_owner(part1, got1, s, send_sem.at[3], phase_recv.at[0])
    wait(got1.at[pl.ds(1, 15)], phase_recv.at[0])
    total = part1[0]
    for s in range(1, 16):
        total = total + got1[s]
    r0 = target - (scale * total + start)
    weight = scale * r0
    vec1[0] = weight
    vec1r[0] = weight

    for s in row_far:
        at = mirror(s)
        send(vec1.at[0], vec1.at[at], row_peer(*SLOTS[s], 0), send_sem.at[4], phase_recv.at[1 if at < 12 else 2])
    send(vec1.at[0], vec1.at[16], sibling, sib_send.at[2], phase_recv.at[3])
    for s in col_far:
        send(vec1r.at[0], vec1r.at[mirror(s)], col_peer(*SLOTS[s]), send_sem.at[5], phase_recv.at[6])

    def second(first, count, fresh, rows):
        add = product(rows, [(first, count)])
        acc[rows, :] = add if fresh else acc[rows, :] + add

    every = pl.ds(0, 1024)
    wait(vec1.at[pl.ds(1, 11)], phase_recv.at[1])
    send(vec1.at[pl.ds(1, 11)], vec1.at[pl.ds(17, 11)], sibling, sib_send.at[2], phase_recv.at[4])
    spread(vec1, 0, 12)
    second(0, 12, True, every)
    wait(vec1.at[pl.ds(12, 4)], phase_recv.at[2])
    send(vec1.at[pl.ds(12, 4)], vec1.at[pl.ds(28, 4)], sibling, sib_send.at[2], phase_recv.at[5])
    spread(vec1, 12, 4)
    second(12, 4, False, every)
    wait(vec1.at[16], phase_recv.at[3])
    wait(vec1.at[pl.ds(17, 11)], phase_recv.at[4])
    spread(vec1, 16, 12)
    second(16, 12, False, every)
    wait(vec1.at[pl.ds(28, 4)], phase_recv.at[5])
    spread(vec1, 28, 4)
    for chunk in (3, 2, 1, 0):
        second(28, 4, False, pl.ds(256 * chunk, 256))
        for s in range(4 * chunk + 3, 4 * chunk - 1, -1):
            to_owner(part2, got2, s, send_sem.at[6], phase_recv.at[7])

    wait(vec1r.at[pl.ds(1, 15)], phase_recv.at[6])
    bend = vec1r[0] * part2[0]
    for s in range(1, 16):
        bend = bend + vec1r[s] * part2[s]
    bend = jnp.sum(bend, axis=0, keepdims=True)
    squares = jnp.sum(r0 * r0, axis=0, keepdims=True)
    leading = lax.broadcasted_iota(jnp.int32, (1, 128), 1) < OUT
    line = jnp.where(leading, fold_lanes(bend), fold_lanes(squares))
    dots[0:1, :] = line
    got_dots[0:1, :] = line
    x = xh * 2 + xl
    at_x = [(x + d) % 4 for d in range(4)]
    rows_x = [(v % 2) * 2 + core for v in at_x]
    cols_x = [v // 2 for v in at_x]
    rows_y = [(y + d) % RING * 4 for d in range(RING)]
    cols_z = [(z + d) % RING * 2 for d in range(RING)]
    for dx, dy, dz in CHIPS:
        back = (-dx % 4 * RING + -dy % RING) * RING + -dz % RING
        to = (rows_y[dy] + rows_x[dx], cols_z[dz] + cols_x[dx])
        send(dots.at[pl.ds(0, 1)], got_dots.at[pl.ds(back, 1)], to, send_sem.at[7], phase_recv.at[8])
    wait(got2.at[pl.ds(1, 15)], phase_recv.at[7])
    total = part2[0]
    for s in range(1, 16):
        total = total + got2[s]
    q = scale * total + r0
    wait(got_dots.at[pl.ds(1, 255)], phase_recv.at[8])
    line = jnp.sum(jnp.sum(got_dots[...].reshape(32, 8, 128), axis=0), axis=0, keepdims=True)
    dots[1:2, :] = line
    send(dots.at[pl.ds(1, 1)], got_dots2.at[pl.ds(0, 1)], sibling, send_sem.at[8], phase_recv.at[9])
    wait(got_dots2.at[pl.ds(0, 1)], phase_recv.at[9])
    line = line + got_dots2[0:1, :]
    bend = fold_lanes(jnp.where(leading, line, 0.0))
    squares = jnp.where(leading, pltpu.roll(line, 128 - OUT, axis=1), line)
    alpha = squares / (bend + squares)
    coef = start + alpha * r0
    res = r0 - alpha * q
    low = lax.broadcasted_iota(jnp.int32, (16, 128), 1) < OUT
    for g in range(4):
        a = pltpu.roll(coef, (128 - OUT * g) % 128, axis=1) if g else coef
        b = pltpu.roll(res, (128 + OUT - OUT * g) % 128, axis=1) if g != 1 else res
        flip[16 * g : 16 * g + 16, :] = jnp.where(low, a, b)
    back = flip[...].T
    both_out[0] = back[0:OUT, 0:SAMP]
    both_out[1] = back[OUT : 2 * OUT, 0:SAMP]

    wait(col_st.at[pl.ds(0, 17)], send_sem.at[0])
    wait(row_st.at[pl.ds(0, 15)], send_sem.at[1])
    wait(col_st.at[pl.ds(0, 14)], sib_send.at[0])
    wait(vec1.at[pl.ds(0, 16)], sib_send.at[2])
    wait(part1.at[pl.ds(0, 15)], send_sem.at[3])
    wait(vec1.at[pl.ds(0, 15)], send_sem.at[4])
    wait(vec1r.at[pl.ds(0, 15)], send_sem.at[5])
    wait(part2.at[pl.ds(0, 15)], send_sem.at[6])
    wait(got_dots.at[pl.ds(0, 255)], send_sem.at[7])
    wait(got_dots2.at[pl.ds(0, 1)], send_sem.at[8])


def store(both, coef_out, res_out, sem):
    copies = [pltpu.make_async_copy(both.at[k], out, sem.at[k]) for k, out in enumerate((coef_out, res_out))]
    for copy in copies:
        copy.start()
    for copy in copies:
        copy.wait()


def local(states, targets, start_coef, washout):
    f32, bf16 = jnp.float32, jnp.bfloat16
    vmem = pl.BlockSpec(memory_space=pltpu.VMEM)
    hbm = pl.BlockSpec(memory_space=pltpu.HBM)
    dma = pltpu.SemaphoreType.DMA
    inputs = (states, targets, start_coef, washout.reshape(1, SAMP))
    both = pl.pallas_call(
        kernel,
        out_shape=pltpu.VMEM((2, OUT, SAMP), f32),
        in_specs=[hbm] * 4,
        out_specs=vmem,
        scratch_shapes=[
            pltpu.VMEM((SAMP, DIM), bf16),
            pltpu.VMEM((2, OUT, SAMP), f32),
            pltpu.VMEM((1, SAMP), jnp.int32),
            pltpu.VMEM((32, COL_SLOT, 128), bf16),
            pltpu.VMEM((16, ROW_SLOT, 128), bf16),
            pltpu.VMEM((1024, 2048), bf16),
            pltpu.VMEM((1024, 2048), bf16),
            pltpu.VMEM((2048, 256), bf16),
            pltpu.VMEM((1024, 128), f32),
            pltpu.VMEM((128, 128), f32),
            pltpu.VMEM((16, 16, 128), f32),
            pltpu.VMEM((16, 16, 128), f32),
            pltpu.VMEM((32, 16, 128), f32),
            pltpu.VMEM((16, 16, 128), f32),
            pltpu.VMEM((16, 16, 128), f32),
            pltpu.VMEM((16, 16, 128), f32),
            pltpu.VMEM((8, 128), f32),
            pltpu.VMEM((256, 128), f32),
            pltpu.VMEM((8, 128), f32),
            dma((4,)),
            dma((9,)),
            dma((3,)),
            dma((18,)),
            dma((8,)),
            dma((18,)),
            dma((10,)),
        ],
        compiler_params=pltpu.CompilerParams(
            collective_id=0, has_side_effects=True, vmem_limit_bytes=48 * 1024 * 1024
        ),
    )(*[pltpu.with_memory_space_constraint(x, pltpu.HBM) for x in inputs])
    out = jax.ShapeDtypeStruct((OUT, SAMP), f32)
    return pl.pallas_call(
        store,
        out_shape=(out, out),
        in_specs=[vmem],
        out_specs=(hbm, hbm),
        scratch_shapes=[dma((2,))],
        compiler_params=pltpu.CompilerParams(vmem_limit_bytes=2 * 1024 * 1024),
    )(both)


def solution(mesh):
    return jax.shard_map(
        local,
        mesh=mesh,
        in_specs=(
            P(("row", "col"), None),
            P(None, ("row", "col")),
            P(None, ("row", "col")),
            P(("row", "col")),
        ),
        out_specs=(P(None, ("row", "col")), P(None, ("row", "col"))),
        check_vma=False,
    )
```

```python
import math

import jax
import jax.numpy as jnp
from jax import lax
from jax.experimental import pallas as pl
from jax.experimental.pallas import tpu as pltpu
from jax.sharding import PartitionSpec as P

MESH = pl.DeviceIdType.MESH
RING = 8
SAMP = 64
DIM = 512
OUT = 32
SLOTS = [
    (0, 0), (0, 1), (-2, 0), (2, 0),
    (-1, 0), (1, 0), (-2, 1), (2, 1), (-3, 0), (3, 0),
    (-1, 1), (1, 1), (-3, 1), (3, 1),
    (4, 0), (4, 1),
]
INDEX = {slot: at for at, slot in enumerate(SLOTS)}
GROUPS = [(0, 4), (4, 6), (10, 4)]
SOONER = 14
ROW_SLOT = 4 * SAMP
COL_SLOT = ROW_SLOT + 32
EXP_SCALE = math.log2(math.e) * 2.0 / DIM


def place(d, a):
    return INDEX[(d + RING // 2 - 1) % RING - RING // 2 + 1, a % 2]


def mirror(s):
    return place(-SLOTS[s][0], SLOTS[s][1])


CHIPS = sorted(
    [(dx, dy, dz) for dx in range(4) for dy in range(RING) for dz in range(RING) if dx or dy or dz],
    key=lambda d: -min(d[0], 4 - d[0]) - min(d[1], RING - d[1]) - min(d[2], RING - d[2]),
)


def far_first(pair_hops):
    return sorted(range(1, 16), key=lambda s: -abs(SLOTS[s][0]) - pair_hops * SLOTS[s][1])


def lane_group():
    return lax.broadcasted_iota(jnp.int32, (16, 128), 1) // OUT


def by_group(pieces):
    group = lane_group()
    out = pieces[3]
    for g in (2, 1, 0):
        out = jnp.where(group == g, pieces[g], out)
    return out


def pack(block, at):
    return by_group(
        [
            pltpu.roll(block[16 * g : 16 * g + 16], (OUT * (g - at)) % 128, axis=1)
            if g != at
            else block[16 * g : 16 * g + 16]
            for g in range(4)
        ]
    )


def fold_lanes(x):
    x = x + pltpu.roll(x, 64, axis=1)
    return x + pltpu.roll(x, 32, axis=1)


def kernel(
    states_in, targets_in, coef_in, washout_in,
    both_out,
    states, vectors, washout, col_st, row_st, e_hi, e_lo, w_all, acc, flip,
    part1, got1, vec1, vec1r, part2, got2, dots, got_dots, got_dots2,
    in_sem, send_sem, sib_send, c_recv, s_recv, r_recv, phase_recv,
):
    row, col = lax.axis_index("row"), lax.axis_index("col")
    core, xl, y = row % 2, (row // 2) % 2, row // 4
    xh, z = col % 2, col // 2

    def row_peer(dy, dxl, dcore):
        return (((y + dy + RING) % RING * 2 + (xl + dxl) % 2) * 2 + (core + dcore) % 2, col)

    def col_peer(dz, dxh):
        return (row, (z + dz + RING) % RING * 2 + (xh + dxh) % 2)

    sibling = row_peer(0, 0, 1)
    near = [row_peer(1, 0, 0), row_peer(-1, 0, 0), row_peer(0, 1, 0), sibling]
    near += [col_peer(1, 0), col_peer(-1, 0), col_peer(0, 1)]
    near += [row_peer(2, 0, 0), row_peer(-2, 0, 0), col_peer(2, 0), col_peer(-2, 0)]

    barrier = pltpu.get_barrier_semaphore()
    for who in near:
        pl.semaphore_signal(barrier, inc=1, device_id=who, device_id_type=MESH)

    fetches = [
        pltpu.make_async_copy(states_in, states, in_sem.at[0]),
        pltpu.make_async_copy(targets_in, vectors.at[0], in_sem.at[1]),
        pltpu.make_async_copy(coef_in, vectors.at[1], in_sem.at[2]),
        pltpu.make_async_copy(washout_in, washout, in_sem.at[3]),
    ]
    for fetch in fetches:
        fetch.start()

    def send(src, dst, to, s_sem, r_sem):
        pltpu.make_async_remote_copy(
            src_ref=src, dst_ref=dst, send_sem=s_sem, recv_sem=r_sem, device_id=to, device_id_type=MESH
        ).start()

    def wait(ref, sem):
        pltpu.make_async_copy(ref, ref, sem).wait()

    def send_col(s, d, a=0, half=None):
        to = place(SLOTS[s][0] - d, SLOTS[s][1] + a)
        rows = pl.ds(0, COL_SLOT) if half is None else pl.ds(half * (COL_SLOT // 2), COL_SLOT // 2)
        sem = 16 + SLOTS[to][1] if half else to
        src = col_st.at[s, rows]
        send(src, col_st.at[to, rows], row_peer(d, a, 0), send_sem.at[0], c_recv.at[sem])
        if half is not None:
            both = s_recv.at[4 + 2 * half + SLOTS[to][1]]
            send(src, col_st.at[16 + to, rows], row_peer(d, a, 1), send_sem.at[0], both)

    def send_row(s, d, a=0, half=None):
        to = place(SLOTS[s][0] - d, SLOTS[s][1] + a)
        rows = pl.ds(0, ROW_SLOT) if half is None else pl.ds(half * (ROW_SLOT // 2), ROW_SLOT // 2)
        sem = 16 + SLOTS[to][1] if half else to
        send(row_st.at[s, rows], row_st.at[to, rows], col_peer(d, a), send_sem.at[1], r_recv.at[sem])

    def take_col(s):
        if SLOTS[s][0] == 4:
            for half in (0, 1):
                rows = pl.ds(half * (COL_SLOT // 2), COL_SLOT // 2)
                wait(col_st.at[s, rows], c_recv.at[16 + SLOTS[s][1] if half else s])
                wait(col_st.at[16 + s, rows], s_recv.at[4 + 2 * half + SLOTS[s][1]])
        else:
            wait(col_st.at[s], c_recv.at[s])

    def take_row(s):
        if SLOTS[s][0] == 4:
            for half in (0, 1):
                rows = pl.ds(half * (ROW_SLOT // 2), ROW_SLOT // 2)
                wait(row_st.at[s, rows], r_recv.at[16 + SLOTS[s][1] if half else s])
        else:
            wait(row_st.at[s], r_recv.at[s])

    def share(g):
        first, count = GROUPS[g]
        own, other = pl.ds(first, count), pl.ds(16 + first, count)
        send(col_st.at[own], col_st.at[other], sibling, sib_send.at[0], s_recv.at[g])

    pl.semaphore_wait(barrier, len(near))
    first_ways = [(0, 1), (2, 0), (-2, 0)]
    for d, a in first_ways:
        to = place(-d, a)
        for k in range(4):
            piece = states_in.at[:, pl.ds(128 * k, 128)]
            rows = pl.ds(SAMP * k, SAMP)
            send(piece, col_st.at[to, rows], row_peer(d, a, 0), send_sem.at[0], c_recv.at[to])
            send(piece, row_st.at[to, rows], col_peer(d, a), send_sem.at[1], r_recv.at[to])
    fetches[0].wait()

    for k in range(4):
        piece = states[:, 128 * k : 128 * k + 128]
        col_st[0, SAMP * k : SAMP * k + SAMP, :] = piece
        row_st[0, SAMP * k : SAMP * k + SAMP, :] = piece
    own_f = states[...].astype(jnp.float32)
    norm = jnp.sum(own_f * own_f, axis=1, keepdims=True)
    damp_col = jnp.broadcast_to(jnp.exp(norm * (-1.0 / DIM)), (SAMP, 128))
    damp = by_group([damp_col[16 * g : 16 * g + 16] for g in range(4)])
    for fetch in fetches[1:]:
        fetch.wait()
    flip[0:OUT, 0:SAMP] = vectors[0]
    flip[OUT : 2 * OUT, 0:SAMP] = vectors[1]
    flip[2 * OUT : 3 * OUT, 0:SAMP] = jnp.broadcast_to(washout[...].astype(jnp.float32), (OUT, SAMP))
    turned = flip[...].T[0:SAMP]
    mask = pack(turned, 2)
    target = pack(turned, 0) * mask
    start = pack(turned, 1)
    scale = mask * damp
    weight = scale * start
    high = weight.astype(jnp.bfloat16)
    col_st[0, ROW_SLOT : ROW_SLOT + 16, :] = high
    col_st[0, ROW_SLOT + 16 : COL_SLOT, :] = (weight - high.astype(jnp.float32)).astype(jnp.bfloat16)
    for d, a in first_ways:
        rows = pl.ds(ROW_SLOT, 32)
        to = place(-d, a)
        send(col_st.at[0, rows], col_st.at[to, rows], row_peer(d, a, 0), send_sem.at[0], c_recv.at[to])

    group = lane_group()

    def lay(s, hi, lo):
        for g in range(4):
            keep = group == g
            at = SAMP * s + 16 * g
            w_all[at : at + 16, 0:128] = jnp.where(keep, hi, 0.0).astype(jnp.bfloat16)
            w_all[at : at + 16, 128:256] = jnp.where(keep, lo, 0.0).astype(jnp.bfloat16)

    def spread_sent(first, count):
        for s in range(first, first + count):
            hi = col_st[s, ROW_SLOT : ROW_SLOT + 16, :]
            lo = col_st[s, ROW_SLOT + 16 : COL_SLOT, :]
            lay(s, hi.astype(jnp.float32), lo.astype(jnp.float32))

    def spread(vec, first, count):
        for s in range(first, first + count):
            hi = vec[s].astype(jnp.bfloat16).astype(jnp.float32)
            lay(s, hi, vec[s] - hi)

    def product(rows, ranges):
        columns = [pl.ds(a * SAMP, k * SAMP) for a, k in ranges]
        hi, lo = [jnp.concatenate([e[rows, c] for c in columns], axis=1) for e in (e_hi, e_lo)]
        w = jnp.concatenate([w_all[c, :] for c in columns], axis=0)
        both = jnp.dot(hi, w, preferred_element_type=jnp.float32)
        low = jnp.dot(lo, w[:, 0:128], preferred_element_type=jnp.float32)
        return both[:, 0:128] + both[:, 128:256] + low

    def slots_of(buf, first, count):
        return jnp.concatenate(
            [
                jnp.concatenate([buf[s, SAMP * k : SAMP * k + SAMP, :] for k in range(4)], axis=1)
                for s in range(first, first + count)
            ],
            axis=0,
        )

    def tile(r_first, r_count, ranges):
        left = slots_of(row_st, r_first, r_count)
        right = jnp.concatenate([slots_of(col_st, a, k) for a, k in ranges], axis=0)
        cross = lax.dot_general(left, right, (((1,), (1,)), ((), ())), preferred_element_type=jnp.float32)
        e = jnp.exp2(cross * EXP_SCALE)
        hi = e.astype(jnp.bfloat16)
        lo = (e - hi.astype(jnp.float32)).astype(jnp.bfloat16)
        rows = pl.ds(r_first * SAMP, r_count * SAMP)
        at = 0
        for a, k in ranges:
            columns = pl.ds(a * SAMP, k * SAMP)
            e_hi[rows, columns] = hi[:, at : at + k * SAMP]
            e_lo[rows, columns] = lo[:, at : at + k * SAMP]
            at += k * SAMP

    def grow_own(g):
        first, count = GROUPS[g]
        if first:
            tile(first, count, [(0, first), (16, first)])
        tile(0, first + count, [(first, count)])

    def grow_other(g):
        first, count = GROUPS[g]
        wait(col_st.at[pl.ds(16 + first, count)], s_recv.at[g])
        tile(0, first + count, [(16 + first, count)])

    sides = (-1, 1)
    pair = place(0, 1)
    chains = ((take_col, send_col), (take_row, send_row))
    for take, pass_on in chains:
        take(pair)
        for side in sides:
            pass_on(pair, 2 * side)
        for side in sides:
            pass_on(0, side)
    for take, pass_on in chains:
        for side in sides:
            take(place(2 * side, 0))
            pass_on(place(2 * side, 0), -side)
    share(0)
    grow_own(0)
    grow_other(0)
    for take, pass_on in chains:
        for side in sides:
            take(place(2 * side, 1))
            pass_on(place(2 * side, 1), -side)
        for side in sides:
            pass_on(pair, side)
    for take, pass_on in chains:
        for side in sides:
            take(place(side, 0))
        for side in sides:
            take(place(3 * side, 0))
            pass_on(place(3 * side, 0), -side, half=(side + 1) // 2)
    share(1)
    grow_own(1)
    grow_other(1)
    for take, pass_on in chains:
        for side in sides:
            take(place(3 * side, 1))
            pass_on(place(3 * side, 1), -side, half=(side + 1) // 2)
        for side in sides:
            take(place(side, 1))
    share(2)
    before = GROUPS[2][0]
    grow_own(2)
    for first in (0, 16):
        spread_sent(first, before)
    for first, count in ((0, 256), (256, 256), (512, 128)):
        rows = pl.ds(first, count)
        acc[rows, :] = product(rows, [(0, before), (16, before)])
    grow_other(2)
    for first in (0, 16):
        spread_sent(first + before, SOONER - before)
    for first, count in ((0, 256), (256, 256), (512, 128)):
        rows = pl.ds(first, count)
        acc[rows, :] += product(rows, [(before, SOONER - before), (16 + before, SOONER - before)])
    rows = pl.ds(before * SAMP, (SOONER - before) * SAMP)
    acc[rows, :] = product(rows, [(0, SOONER), (16, SOONER)])
    for a in (0, 1):
        take_col(place(4, a))

    row_far, col_far = far_first(1), far_first(2)

    def to_owner(part, got, s, s_sem, r_sem):
        whole = fold_lanes(acc[SAMP * s : SAMP * s + SAMP, :])
        part[s] = by_group([whole[16 * g : 16 * g + 16] for g in range(4)])
        if s:
            send(part.at[s], got.at[mirror(s)], col_peer(*SLOTS[s]), s_sem, r_sem)

    last = [(SOONER, 2), (16 + SOONER, 2)]
    spread_sent(SOONER, 2)
    spread_sent(16 + SOONER, 2)
    for a in (0, 1):
        take_row(place(4, a))
    tile(SOONER, 2, [(0, 32)])
    for first, count in ((14, 2), (10, 4), (6, 4), (4, 2), (0, 4)):
        rows = pl.ds(first * SAMP, count * SAMP)
        if first == SOONER:
            acc[rows, :] = product(rows, [(0, 32)])
        else:
            tile(first, count, last)
            acc[rows, :] += product(rows, last)
        for s in range(first + count - 1, first - 1, -1):
            to_owner(part1, got1, s, send_sem.at[3], phase_recv.at[0])
    wait(got1.at[pl.ds(1, 15)], phase_recv.at[0])
    total = part1[0]
    for s in range(1, 16):
        total = total + got1[s]
    r0 = target - (scale * total + start)
    weight = scale * r0
    vec1[0] = weight
    vec1r[0] = weight

    for s in row_far:
        at = mirror(s)
        send(vec1.at[0], vec1.at[at], row_peer(*SLOTS[s], 0), send_sem.at[4], phase_recv.at[1 if at < 12 else 2])
    send(vec1.at[0], vec1.at[16], sibling, sib_send.at[2], phase_recv.at[3])
    for s in col_far:
        send(vec1r.at[0], vec1r.at[mirror(s)], col_peer(*SLOTS[s]), send_sem.at[5], phase_recv.at[6])

    def second(first, count, fresh, rows):
        add = product(rows, [(first, count)])
        acc[rows, :] = add if fresh else acc[rows, :] + add

    every = pl.ds(0, 1024)
    wait(vec1.at[pl.ds(1, 11)], phase_recv.at[1])
    send(vec1.at[pl.ds(1, 11)], vec1.at[pl.ds(17, 11)], sibling, sib_send.at[2], phase_recv.at[4])
    spread(vec1, 0, 12)
    second(0, 12, True, every)
    wait(vec1.at[pl.ds(12, 4)], phase_recv.at[2])
    send(vec1.at[pl.ds(12, 4)], vec1.at[pl.ds(28, 4)], sibling, sib_send.at[2], phase_recv.at[5])
    spread(vec1, 12, 4)
    second(12, 4, False, every)
    wait(vec1.at[16], phase_recv.at[3])
    wait(vec1.at[pl.ds(17, 11)], phase_recv.at[4])
    spread(vec1, 16, 12)
    second(16, 12, False, every)
    wait(vec1.at[pl.ds(28, 4)], phase_recv.at[5])
    spread(vec1, 28, 4)
    for chunk in (3, 2, 1, 0):
        second(28, 4, False, pl.ds(256 * chunk, 256))
        for s in range(4 * chunk + 3, 4 * chunk - 1, -1):
            to_owner(part2, got2, s, send_sem.at[6], phase_recv.at[7])

    wait(vec1r.at[pl.ds(1, 15)], phase_recv.at[6])
    bend = vec1r[0] * part2[0]
    for s in range(1, 16):
        bend = bend + vec1r[s] * part2[s]
    bend = jnp.sum(bend, axis=0, keepdims=True)
    squares = jnp.sum(r0 * r0, axis=0, keepdims=True)
    leading = lax.broadcasted_iota(jnp.int32, (1, 128), 1) < OUT
    line = jnp.where(leading, fold_lanes(bend), fold_lanes(squares))
    dots[0:1, :] = line
    got_dots[0:1, :] = line
    x = xh * 2 + xl
    at_x = [(x + d) % 4 for d in range(4)]
    rows_x = [(v % 2) * 2 + core for v in at_x]
    cols_x = [v // 2 for v in at_x]
    rows_y = [(y + d) % RING * 4 for d in range(RING)]
    cols_z = [(z + d) % RING * 2 for d in range(RING)]
    for dx, dy, dz in CHIPS:
        back = (-dx % 4 * RING + -dy % RING) * RING + -dz % RING
        to = (rows_y[dy] + rows_x[dx], cols_z[dz] + cols_x[dx])
        send(dots.at[pl.ds(0, 1)], got_dots.at[pl.ds(back, 1)], to, send_sem.at[7], phase_recv.at[8])
    wait(got_dots.at[pl.ds(1, 255)], phase_recv.at[8])
    line = jnp.sum(jnp.sum(got_dots[...].reshape(32, 8, 128), axis=0), axis=0, keepdims=True)
    dots[1:2, :] = line
    send(dots.at[pl.ds(1, 1)], got_dots2.at[pl.ds(0, 1)], sibling, send_sem.at[8], phase_recv.at[9])
    wait(got2.at[pl.ds(1, 15)], phase_recv.at[7])
    total = part2[0]
    for s in range(1, 16):
        total = total + got2[s]
    q = scale * total + r0
    wait(got_dots2.at[pl.ds(0, 1)], phase_recv.at[9])
    line = line + got_dots2[0:1, :]
    bend = fold_lanes(jnp.where(leading, line, 0.0))
    squares = jnp.where(leading, pltpu.roll(line, 128 - OUT, axis=1), line)
    alpha = squares / (bend + squares)
    coef = start + alpha * r0
    res = r0 - alpha * q
    low = lax.broadcasted_iota(jnp.int32, (16, 128), 1) < OUT
    for g in range(4):
        a = pltpu.roll(coef, (128 - OUT * g) % 128, axis=1) if g else coef
        b = pltpu.roll(res, (128 + OUT - OUT * g) % 128, axis=1) if g != 1 else res
        flip[16 * g : 16 * g + 16, :] = jnp.where(low, a, b)
    back = flip[...].T
    both_out[0] = back[0:OUT, 0:SAMP]
    both_out[1] = back[OUT : 2 * OUT, 0:SAMP]

    wait(col_st.at[pl.ds(0, 17)], send_sem.at[0])
    wait(row_st.at[pl.ds(0, 15)], send_sem.at[1])
    wait(col_st.at[pl.ds(0, 14)], sib_send.at[0])
    wait(vec1.at[pl.ds(0, 16)], sib_send.at[2])
    wait(part1.at[pl.ds(0, 15)], send_sem.at[3])
    wait(vec1.at[pl.ds(0, 15)], send_sem.at[4])
    wait(vec1r.at[pl.ds(0, 15)], send_sem.at[5])
    wait(part2.at[pl.ds(0, 15)], send_sem.at[6])
    wait(got_dots.at[pl.ds(0, 255)], send_sem.at[7])
    wait(got_dots2.at[pl.ds(0, 1)], send_sem.at[8])


def store(both, coef_out, res_out, sem):
    copies = [pltpu.make_async_copy(both.at[k], out, sem.at[k]) for k, out in enumerate((coef_out, res_out))]
    for copy in copies:
        copy.start()
    for copy in copies:
        copy.wait()


def local(states, targets, start_coef, washout):
    f32, bf16 = jnp.float32, jnp.bfloat16
    vmem = pl.BlockSpec(memory_space=pltpu.VMEM)
    hbm = pl.BlockSpec(memory_space=pltpu.HBM)
    dma = pltpu.SemaphoreType.DMA
    inputs = (states, targets, start_coef, washout.reshape(1, SAMP))
    both = pl.pallas_call(
        kernel,
        out_shape=pltpu.VMEM((2, OUT, SAMP), f32),
        in_specs=[hbm] * 4,
        out_specs=vmem,
        scratch_shapes=[
            pltpu.VMEM((SAMP, DIM), bf16),
            pltpu.VMEM((2, OUT, SAMP), f32),
            pltpu.VMEM((1, SAMP), jnp.int32),
            pltpu.VMEM((32, COL_SLOT, 128), bf16),
            pltpu.VMEM((16, ROW_SLOT, 128), bf16),
            pltpu.VMEM((1024, 2048), bf16),
            pltpu.VMEM((1024, 2048), bf16),
            pltpu.VMEM((2048, 256), bf16),
            pltpu.VMEM((1024, 128), f32),
            pltpu.VMEM((128, 128), f32),
            pltpu.VMEM((16, 16, 128), f32),
            pltpu.VMEM((16, 16, 128), f32),
            pltpu.VMEM((32, 16, 128), f32),
            pltpu.VMEM((16, 16, 128), f32),
            pltpu.VMEM((16, 16, 128), f32),
            pltpu.VMEM((16, 16, 128), f32),
            pltpu.VMEM((8, 128), f32),
            pltpu.VMEM((256, 128), f32),
            pltpu.VMEM((8, 128), f32),
            dma((4,)),
            dma((9,)),
            dma((3,)),
            dma((18,)),
            dma((8,)),
            dma((18,)),
            dma((10,)),
        ],
        compiler_params=pltpu.CompilerParams(
            collective_id=0, has_side_effects=True, vmem_limit_bytes=48 * 1024 * 1024
        ),
    )(*[pltpu.with_memory_space_constraint(x, pltpu.HBM) for x in inputs])
    out = jax.ShapeDtypeStruct((OUT, SAMP), f32)
    return pl.pallas_call(
        store,
        out_shape=(out, out),
        in_specs=[vmem],
        out_specs=(hbm, hbm),
        scratch_shapes=[dma((2,))],
        compiler_params=pltpu.CompilerParams(vmem_limit_bytes=2 * 1024 * 1024),
    )(both)


def solution(mesh):
    return jax.shard_map(
        local,
        mesh=mesh,
        in_specs=(
            P(("row", "col"), None),
            P(None, ("row", "col")),
            P(None, ("row", "col")),
            P(("row", "col")),
        ),
        out_specs=(P(None, ("row", "col")), P(None, ("row", "col"))),
        check_vma=False,
    )
```
